128 devices in a mesh: grp: 4 (over z), shard: 32 (over x, y, core).
Axes of the slice: x: 4, y: 4, z: 4, core: 2. Of those that a mesh axis runs over, the one named last changes fastest.
Arguments:
- latents: bfloat16 [16384, 1024], P(('grp', 'shard')), may hold values from -24 to 24
- head_weight: bfloat16 [1024, 1024], P('shard'), may hold values from -0.1875 to 0.1875
- norm_gain: float32 [1024], replicated, may hold values from 0.1 to 1.9
- color_head: bfloat16 [4, 256], replicated, may hold values from -1.5 to 1.5
- sample_points: float32 [8192, 192], P(('grp', 'shard')), may hold values from -1 to 1
- sample_spacing: float32 [8192, 64], P(('grp', 'shard')), may hold values from 0.002 to 0.02
- ray_targets: float32 [3, 8192], P(None, ('grp', 'shard')), may hold values from 0 to 1
- ray_scene: int32 [8192], P(('grp', 'shard')), may hold values from 0 to 127, as said below
Outputs:
- rendered_color: float32 [3, 8192], P(None, ('grp', 'shard'))
- loss: float32 [], replicated
- head_grad: float32 [1024, 1024], P('shard')
- norm_gain_grad: float32 [1024], replicated
- latent_grad: bfloat16 [16384, 1024], P(('grp', 'shard'))
The draws below stay inside these ranges and needn't reach their ends.
Inputs may be any that keep to these rules, and one draw needn't show every extreme that they name: `ray_scene`: one scene, drawn from the seed, is named by exactly 2 rays of every device; no device names any scene more than 2 times; every scene is named by one ray or more, and the totals of the other scenes differ from one another by one at most.
All inputs are finite; a program needn't handle non-finite values.
Results may differ from the reference program's by a relative error of at most 0.017.
Values may be sent and summed in bfloat16 or wider, within the bound.
No kernel may reach another device: no remote copies, remote signals or barrier semaphores. Data moves between devices by JAX's collectives and lax.ppermute only.
A program may use at most 64 MiB of HBM per device.

```python
import math
import jax
import jax.numpy as jnp
from jax import lax

D = 1024
WF = 256
LAYERS = 2
RS = 64
RAY_DEV = 64
LAT = 128
SCENES = 128
RAYS = 8192
DEVICES = 128


def draw_ray_scene(key, part):
    key_hot, key_rest, key_turn, key_place = jax.random.split(jax.random.fold_in(key, 11), 4)
    hot_scene = jax.random.randint(key_hot, (), 0, SCENES)
    others = jax.random.permutation(key_rest, SCENES - 1).astype(jnp.int32)
    others = others + (others >= hot_scene).astype(jnp.int32)
    offset_turn = jax.random.randint(key_turn, (), 0, SCENES - 1)
    places = jax.random.split(key_place, DEVICES)
    shuffled = jax.vmap(lambda place_key: jax.random.permutation(place_key, RAY_DEV))(places)
    ray_rank = jnp.argsort(shuffled, axis=1, stable=True).astype(jnp.int32)
    per_device = 4 * RAY_DEV // DEVICES
    device_ids = jnp.arange(DEVICES, dtype=jnp.int32)[:, None]
    position = jnp.remainder(offset_turn + device_ids * (RAY_DEV - per_device) + ray_rank - per_device, SCENES - 1)
    scene_ids = jnp.where(ray_rank < per_device, hot_scene, others[position])
    return scene_ids.reshape(RAYS).astype(jnp.int32)


def strengthened(array, stream_key, source, target, blocks, factor):
    def block_of(axis_at):
        return (jnp.arange(array.shape[axis_at]) // (array.shape[axis_at] // blocks)).reshape((-1,) + (1,) * (array.ndim - 1 - axis_at))

    one_side = jax.random.permutation(stream_key, blocks)[block_of(target)]
    other_side = (block_of(target) + blocks // 2) % blocks
    return jnp.where((block_of(source) == one_side) | (block_of(source) == other_side), factor * array, array)


def shard_levels(stream_key, shape, shards, low, largest):
    loudness = 1.0
    for axis_at, shards_of in shards:
        steps = jax.random.uniform(jax.random.fold_in(jax.random.fold_in(stream_key, 6), axis_at), (shards_of,), jnp.float32, low / len(shards), largest / len(shards))
        loudness = loudness * jnp.repeat(jnp.exp(steps), shape[axis_at] // shards_of).reshape((-1,) + (1,) * (len(shape) - 1 - axis_at))
    return loudness


def gaussian(own_key, shape, spread, bound, cuts=(), held_as=jnp.bfloat16):
    factor_of = shard_levels(own_key, shape, cuts, -0.22, 0.18) if cuts else 1.0
    result = jax.random.normal(own_key, shape, jnp.float32) * spread * factor_of
    return jnp.minimum(jnp.maximum(result, -bound), bound).astype(held_as)


def noise_with(rng, shape, scale, bound, pieces, heavy, kind=jnp.bfloat16):
    array = scale * jax.random.normal(rng, shape, jnp.float32)
    if pieces:
        array = array * shard_levels(rng, shape, pieces, -0.22, 0.18)
    return jnp.clip(strengthened(array, jax.random.fold_in(rng, 3), *heavy), -bound, bound).astype(kind)


def setup_inputs(seed: int = 0) -> dict:
    key_list = jax.random.split(jax.random.key(seed), 9)
    return {
        "latents": noise_with(key_list[0], (SCENES * LAT, D), 1.0, 24.0, ((0, 128),), (0, 1, 128, 5.5)),
        "head_weight": gaussian(key_list[1], (D, D), D ** -0.5, 0.1875, ((0, 32),)),
        "norm_gain": jnp.clip(1.0 + 0.18 * jax.random.normal(key_list[2], (D,), jnp.float32), 0.1, 1.9),
        "color_head": gaussian(key_list[3], (4, WF), (WF // 16) ** -0.5, 1.5),
        "sample_points": jnp.clip(jax.random.uniform(key_list[4], (RAYS, 3 * RS), jnp.float32, -1.0, 1.0) * shard_levels(key_list[4], (RAYS, 3 * RS), ((0, 128),), -0.4, 0.0), -1.0, 1.0),
        "sample_spacing": jnp.clip(jnp.exp(math.log(0.02) - 2.30258502 * jax.random.uniform(key_list[5], (RAYS, RS), jnp.float32) ** shard_levels(key_list[5], (RAYS, RS), ((0, 128),), -0.2, 0.2)), 0.002, 0.02),
        "ray_targets": jnp.clip(1.0 * jax.random.uniform(key_list[6], (3, RAYS), jnp.float32) ** shard_levels(key_list[6], (3, RAYS), ((1, 128),), -0.2, 0.2), 0.0, 1.0),
        "ray_scene": draw_ray_scene(jax.random.fold_in(key_list[8], 71), 0),
    }


norm_eps = 1e-06

def encode(sample_rows, field_width):
    column = jnp.arange(field_width)
    component = column % 3
    octave = (column // 6 % 8).astype(jnp.float32)
    frequency = jnp.exp2(octave) * math.pi
    phase_shift = (column // 3 % 2).astype(jnp.float32) * (0.5 * math.pi)
    picked = jnp.zeros((sample_rows.shape[0], field_width), jnp.float32)
    for coord in range(3):
        chosen = (component == coord).astype(jnp.float32)
        picked = picked + sample_rows[:, coord:coord + 1] * chosen[None, :]
    return jnp.sin(picked * frequency + phase_shift)

def point_rows(points, ray_depth):
    ray_number = points.shape[0]
    return points.reshape(ray_number, 3, ray_depth).transpose(0, 2, 1).reshape(ray_number * ray_depth, 3)

def render_rays(points, spacing, target, live_rays, scene_factor, w_first, w_second, color_head):
    ray_number, ray_depth = spacing.shape
    field_width = w_first.shape[0]
    fan_scale = field_width ** (-0.5)
    sample_rows = point_rows(points, ray_depth)
    h_zero = encode(sample_rows, field_width).astype(jnp.bfloat16)
    h_one = jax.nn.relu(jnp.dot(h_zero, w_first, preferred_element_type=jnp.float32) * fan_scale).astype(jnp.bfloat16)
    h_two = jax.nn.relu(jnp.dot(h_one, w_second, preferred_element_type=jnp.float32) * fan_scale).astype(jnp.bfloat16)
    raw_out = lax.dot_general(color_head, h_two, (((1,), (1,)), ((), ())), preferred_element_type=jnp.float32)
    density = jax.nn.softplus(raw_out[0]).reshape(ray_number, ray_depth)
    albedo = jax.nn.sigmoid(raw_out[1:4]).reshape(3, ray_number, ray_depth)
    optical = density * spacing
    optical_before = jnp.cumsum(optical, axis=1) - optical
    transmit = jnp.exp(-optical_before)
    survive = jnp.exp(-optical)
    blend = transmit * (1.0 - survive)
    ray_color = lax.optimization_barrier(jnp.sum(blend[None] * (albedo - 1.0), axis=2)) + 1.0
    residual = ray_color - target.T
    loss_part = jnp.sum(jnp.where(live_rays, lax.optimization_barrier(jnp.sum(residual * residual, axis=0)) * scene_factor, 0.0))
    grad_color = jnp.where(live_rays[None, :], 2.0 * residual * scene_factor, 0.0)
    d_albedo = grad_color[:, :, None] * blend[None]
    d_blend = lax.optimization_barrier(jnp.sum(grad_color[:, :, None] * (albedo - 1.0), axis=0))
    weighted = d_blend * blend
    behind = lax.optimization_barrier(jnp.sum(weighted, axis=1, keepdims=True)) - jnp.cumsum(weighted, axis=1)
    d_optical = d_blend * transmit * survive - behind
    d_density = (d_optical * spacing * jax.nn.sigmoid(raw_out[0]).reshape(ray_number, ray_depth)).reshape(1, ray_number * ray_depth)
    d_tint = (d_albedo * albedo * (1.0 - albedo)).reshape(3, ray_number * ray_depth)
    d_raw = jnp.concatenate([d_density, d_tint], axis=0).astype(jnp.bfloat16)
    d_htwo = lax.dot_general(d_raw, color_head, (((0,), (0,)), ((), ())), preferred_element_type=jnp.float32)
    d_atwo = (jnp.where(h_two > 0, d_htwo, 0.0) * fan_scale).astype(jnp.bfloat16)
    grad_second = lax.dot_general(h_one, d_atwo, (((0,), (0,)), ((), ())), preferred_element_type=jnp.float32)
    d_hone = lax.dot_general(d_atwo, w_second, (((1,), (1,)), ((), ())), preferred_element_type=jnp.float32)
    d_aone = (jnp.where(h_one > 0, d_hone, 0.0) * fan_scale).astype(jnp.bfloat16)
    grad_first = lax.dot_general(h_zero, d_aone, (((0,), (0,)), ((), ())), preferred_element_type=jnp.float32)
    return (ray_color, loss_part, grad_first, grad_second)

def reference(latents, head_weight, norm_gain, color_head, sample_points, sample_spacing, ray_targets, ray_scene):
    field_width = color_head.shape[1]
    ray_total, ray_depth = sample_spacing.shape
    latent_f32 = latents.astype(jnp.float32)
    inv_rms = lax.rsqrt(lax.optimization_barrier(jnp.mean(latent_f32 * latent_f32, axis=1, keepdims=True)) + norm_eps)
    x_hat = latent_f32 * inv_rms
    x_norm = (x_hat * norm_gain).astype(jnp.bfloat16)
    field_rows = jnp.dot(x_norm, head_weight, preferred_element_type=jnp.float32).astype(jnp.bfloat16)
    field_layers = field_rows.reshape(SCENES, LAYERS, field_width, field_width)
    scene_ids = jnp.arange(SCENES, dtype=jnp.int32)
    counts = lax.optimization_barrier(jnp.sum((ray_scene[:, None] == scene_ids[None, :]).astype(jnp.int32), axis=0))
    offsets = (jnp.cumsum(counts) - counts).astype(jnp.int32)
    sort_order = jnp.argsort(ray_scene, stable=True)
    inverse = jnp.argsort(sort_order, stable=True)
    sub_rays = RAY_DEV
    points_sorted = jnp.concatenate([sample_points[sort_order], jnp.zeros((sub_rays, sample_points.shape[1]), jnp.float32)], axis=0)
    spacing_sorted = jnp.concatenate([sample_spacing[sort_order], jnp.zeros((sub_rays, ray_depth), jnp.float32)], axis=0)
    target_sorted = jnp.concatenate([ray_targets.T[sort_order], jnp.zeros((sub_rays, 3), jnp.float32)], axis=0)

    def per_scene(running, scene_item):
        colors, loss_sum = running
        weights_pair, scene_rays, offset = scene_item
        scene_factor = 1.0 / (SCENES * scene_rays.astype(jnp.float32))
        w_first = weights_pair[0]
        w_second = weights_pair[1]

        def per_block(block_index, inner):
            grad_first, grad_second, colors, loss_sum = inner
            first_row = (offset + block_index * sub_rays).astype(jnp.int32)
            points = lax.dynamic_slice_in_dim(points_sorted, first_row, sub_rays, 0)
            spacing = lax.dynamic_slice_in_dim(spacing_sorted, first_row, sub_rays, 0)
            target = lax.dynamic_slice_in_dim(target_sorted, first_row, sub_rays, 0)
            live_rays = block_index * sub_rays + jnp.arange(sub_rays, dtype=jnp.int32) < scene_rays
            ray_color, loss_part, more_first, more_second = render_rays(points, spacing, target, live_rays, scene_factor, w_first, w_second, color_head)
            previous = lax.dynamic_slice_in_dim(colors, first_row, sub_rays, 1)
            colors = lax.dynamic_update_slice_in_dim(colors, jnp.where(live_rays[None, :], ray_color, previous), first_row, 1)
            return (grad_first + more_first, grad_second + more_second, colors, loss_sum + loss_part)
        zero_grad = jnp.zeros((field_width, field_width), jnp.float32)
        block_count = ((scene_rays + sub_rays - 1) // sub_rays).astype(jnp.int32)
        grad_first, grad_second, colors, loss_sum = lax.fori_loop(jnp.int32(0), block_count, per_block, (zero_grad, zero_grad, colors, loss_sum))
        return ((colors, loss_sum), jnp.stack([grad_first, grad_second]))
    start_colors = jnp.zeros((3, ray_total + sub_rays), jnp.float32)
    (colors, loss_sum), grad_layers = lax.scan(per_scene, (start_colors, jnp.zeros((), jnp.float32)), (field_layers, counts, offsets))
    rendered_color = colors[:, :ray_total][:, inverse]
    d_field = grad_layers.reshape(SCENES * LAT, D).astype(jnp.bfloat16)
    head_grad = lax.dot_general(x_norm, d_field, (((0,), (0,)), ((), ())), preferred_element_type=jnp.float32)
    d_norm = lax.dot_general(d_field, head_weight, (((1,), (1,)), ((), ())), preferred_element_type=jnp.float32)
    norm_gain_grad = lax.optimization_barrier(jnp.sum(d_norm * x_hat, axis=0))
    d_scaled = d_norm * norm_gain
    latent_grad = (inv_rms * (d_scaled - x_hat * lax.optimization_barrier(jnp.mean(d_scaled * x_hat, axis=1, keepdims=True)))).astype(jnp.bfloat16)
    return (rendered_color, loss_sum, head_grad, norm_gain_grad, latent_grad)
```

```python
import jax
import jax.numpy as jnp
import numpy as np
from jax import lax
from jax.experimental import pallas as pl
from jax.experimental.pallas import tpu as pltpu
from jax.sharding import PartitionSpec as P

norm_eps = 1e-06
f32, bf16 = jnp.float32, jnp.bfloat16
both = ("grp", "shard")

sin_coef = (3.141590256747904, -5.167405766362, 2.544000216186916, -0.5594350008327638)
cos_coef = (0.999999953027512, -4.934792802489427, 4.058410790762133, -1.3318729727851486, 0.21968242357146)

step_block = 8
features = 48


def fold_matrix():
    fold = np.zeros((features, 256), np.float32)
    for j in range(256):
        jm = j % features
        m = (jm % 3) * 16 + (jm // 3 % 2) * 8 + jm // 6
        fold[m, (j % 4) * 64 + j // 4] = 1.0
    return fold


def dot(a, b, dims=(((1,), (0,)), ((), ())), precision=None):
    return lax.dot_general(a, b, dims, preferred_element_type=f32, precision=precision)


def pack_kernel(scene_ref, points_ref, spacing_ref, target_ref, out_ref, slot_ref, count_ref, pay_ref, tint_ref):
    rays = points_ref.shape[0]
    for d in range(count_ref.shape[0]):
        count_ref[d] = 0
    out_ref[...] = jnp.zeros_like(out_ref)
    pay_ref[:, 0:192] = points_ref[...]
    pay_ref[:, 192:256] = spacing_ref[...]
    target = jnp.concatenate([target_ref[...], jnp.zeros((5, rays), f32)], axis=0).T
    lane = lax.broadcasted_iota(jnp.int32, (rays, 128), 1)
    for k in range(2):
        placed = jnp.zeros((rays, 128), f32)
        for c in range(3):
            placed = jnp.where(lane == 3 * k + c, target[:, c : c + 1], placed)
        tint_ref[k] = placed

    for r in range(rays):
        scene = scene_ref[r]
        rank = count_ref[scene]
        count_ref[scene] = rank + 1
        slot_ref[r] = scene * 2 + rank
        out_ref[scene, :, pl.ds(pl.multiple_of(rank * 256, 256), 256)] = pay_ref[r : r + 1, :]
        out_ref[scene, :, 512:640] += tint_ref[rank, r : r + 1, :]


def pack(ray_scene, points, spacing, targets, slots):
    rays = points.shape[0]
    return pl.pallas_call(
        pack_kernel,
        out_shape=(
            jax.ShapeDtypeStruct((slots, 1, 640), f32),
            jax.ShapeDtypeStruct((rays,), jnp.int32),
        ),
        in_specs=[pl.BlockSpec(memory_space=pltpu.SMEM)] + [pl.BlockSpec(memory_space=pltpu.VMEM)] * 3,
        out_specs=(pl.BlockSpec(memory_space=pltpu.VMEM), pl.BlockSpec(memory_space=pltpu.SMEM)),
        scratch_shapes=[
            pltpu.SMEM((slots,), jnp.int32),
            pltpu.VMEM((rays, 256), f32),
            pltpu.VMEM((2, rays, 128), f32),
        ],
        cost_estimate=pl.CostEstimate(flops=200000, bytes_accessed=1000000, transcendentals=0),
        name="pack",
    )(ray_scene, points, spacing, targets)


def horner(u, coef):
    value = coef[-1] * u + coef[-2]
    for c in coef[-3::-1]:
        value = value * u + c
    return value


def render_kernel(
    core_ref,
    latent_ref,
    weight_ref,
    gain_ref,
    head_ref,
    recv_ref,
    fold_ref,
    unfold_ref,
    color_ref,
    dfield_ref,
    keep_ref,
    send_ref,
    rays_ref,
    h0_ref,
    h1_ref,
    h2_ref,
    raw_ref,
    draw_ref,
    g0_ref,
    g1_ref,
    rows_ref,
    xnt_ref,
):
    scale = 1.0 / 16.0
    slots = recv_ref.shape[0]
    rays = 2 * slots
    wide = step_block * rays
    blocks = 64 // step_block

    for k in range(2):
        rays_ref[0:256, k * slots : (k + 1) * slots] = recv_ref[:, k * 256 : (k + 1) * 256].T
    tint = recv_ref[:, 512:640].T

    latent = latent_ref[...].astype(f32)
    inv_rms = lax.rsqrt(jnp.mean(latent * latent, axis=1, keepdims=True) + norm_eps)
    normed = latent * inv_rms * gain_ref[...]
    xnt_ref[...] = normed.T.astype(bf16)
    field = dot(normed.astype(bf16), weight_ref[...]).astype(bf16)
    stacked = jnp.concatenate([field[0:64, q * 256 : (q + 1) * 256] for q in range(4)], axis=0)
    folded = dot(fold_ref[...], stacked) * scale
    high = folded.astype(bf16).astype(f32)
    split = jnp.concatenate([high, folded - high, jnp.zeros((32, 256), f32)], axis=0)
    w0t = split.T.astype(bf16)[:, 0:96]
    field1 = field[64:128, :].astype(f32) * scale
    for q in range(4):
        for n in range(2):
            rows_ref[n, pl.ds(q, 64, stride=4), :] = field1[:, q * 256 + n * 128 : q * 256 + (n + 1) * 128]
    w1f = jnp.concatenate([rows_ref[0], rows_ref[1]], axis=1)
    w1 = w1f.astype(bf16)
    w1t = w1f.T.astype(bf16)
    head_f = jnp.concatenate([head_ref[...].astype(f32), jnp.zeros((4, 256), f32)], axis=0)
    head = head_f.astype(bf16)
    head_t = (head_f * scale).T.astype(bf16)

    octave = jnp.left_shift(1, lax.broadcasted_iota(jnp.int32, (8, rays), 0)).astype(f32)

    def forward(b, carry):
        parts = [[] for _ in range(6)]
        for c in range(3):
            group = rays_ref[pl.ds(pl.multiple_of(c * 64 + b * step_block, 8), step_block), :]
            for s in range(step_block):
                y = group[s : s + 1, :] * octave
                whole = jnp.floor(y + 0.5)
                r = y - whole
                half = whole * 0.5
                sign = 1.0 - 4.0 * (half - jnp.floor(half))
                u = r * r
                parts[2 * c].append(r * sign * horner(u, sin_coef))
                parts[2 * c + 1].append(sign * horner(u, cos_coef))
        h0 = jnp.concatenate([jnp.concatenate(p, axis=1) for p in parts], axis=0).astype(bf16)
        h0_ref[b] = h0
        h1 = jnp.maximum(dot(w0t, jnp.concatenate([h0, h0], axis=0)), 0.0).astype(bf16)
        h1_ref[b] = h1
        h2 = jnp.maximum(dot(w1t, h1), 0.0).astype(bf16)
        h2_ref[b] = h2
        raw = dot(head, h2)
        for s in range(step_block):
            at = pl.ds(pl.multiple_of((b * step_block + s) * 8, 8), 8)
            for k in range(2):
                raw_ref[k, at, :] = raw[:, (2 * s + k) * slots : (2 * s + k + 1) * slots]
        return carry

    lax.fori_loop(0, blocks, forward, 0)

    def spread(c):
        return jnp.concatenate([raw_ref[k, pl.ds(c, 64, stride=8), :] for k in range(2)], axis=1)

    def store_gradient(c, value):
        for k in range(2):
            draw_ref[k, pl.ds(c, 64, stride=8), :] = value[:, k * slots : (k + 1) * slots]

    spacing = rays_ref[192:256, :]
    row = lax.broadcasted_iota(jnp.int32, (64, 64), 0)
    column = lax.broadcasted_iota(jnp.int32, (64, 64), 1)
    raw0 = spread(0)
    density = jnp.maximum(raw0, 0.0) + jnp.log1p(jnp.exp(-jnp.abs(raw0)))
    optical = density * spacing
    before = dot((column < row).astype(f32), optical, precision=lax.Precision.HIGHEST)
    transmit = jnp.exp(-before)
    survive = jnp.exp(-optical)
    blend = transmit * (1.0 - survive)
    live = (spacing[0:1, :] > 0.0).astype(f32)
    factor = 1.0 / (float(slots) * jnp.sum(live, axis=1, keepdims=True))
    albedo = [jax.nn.sigmoid(spread(1 + c)) for c in range(3)]
    d_blend = jnp.zeros_like(blend)
    square = jnp.zeros_like(live)
    colors, grads = [], []
    for c in range(3):
        color = jnp.sum(blend * (albedo[c] - 1.0), axis=0, keepdims=True) + 1.0
        target = jnp.concatenate([tint[c : c + 1, :], tint[3 + c : 4 + c, :]], axis=1)
        residual = (color - target) * live
        square = square + residual * residual
        grad = 2.0 * residual * factor
        d_blend = d_blend + grad * (albedo[c] - 1.0)
        colors.append(color)
        grads.append(grad)
    loss = jnp.sum(square, axis=1, keepdims=True) * factor
    rows = [colors[c][:, k * slots : (k + 1) * slots] for k in range(2) for c in range(3)]
    rows += [jnp.broadcast_to(loss, (1, slots)), jnp.zeros((slots - 7, slots), f32)]
    color_ref[...] = jnp.concatenate(rows, axis=0).T
    weighted = d_blend * blend
    behind = dot((column > row).astype(f32), weighted, precision=lax.Precision.HIGHEST)
    d_optical = d_blend * transmit * survive - behind
    draw_ref[...] = jnp.zeros_like(draw_ref)
    store_gradient(0, d_optical * spacing * jax.nn.sigmoid(raw0))
    for c in range(3):
        store_gradient(1 + c, grads[c] * blend * albedo[c] * (1.0 - albedo[c]))

    g0_ref[...] = jnp.zeros_like(g0_ref)
    g1_ref[...] = jnp.zeros_like(g1_ref)
    on_lanes = (((1,), (1,)), ((), ()))

    def backward(b, carry):
        d_raw = jnp.concatenate(
            [
                draw_ref[k, pl.ds(pl.multiple_of((b * step_block + s) * 8, 8), 8), :]
                for s in range(step_block)
                for k in range(2)
            ],
            axis=1,
        ).astype(bf16)
        h1 = h1_ref[b]
        d_a2 = jnp.where(h2_ref[b] > 0, dot(head_t, d_raw).astype(bf16), jnp.zeros((), bf16))
        d_a1 = jnp.where(h1 > 0, dot(w1, d_a2).astype(bf16), jnp.zeros((), bf16))
        g1_ref[...] += dot(h1, d_a2, on_lanes)
        g0_ref[...] += dot(h0_ref[b], d_a1, on_lanes)
        return carry

    lax.fori_loop(0, blocks, backward, 0)

    g0 = dot(unfold_ref[...], g0_ref[...].astype(bf16)).astype(bf16)
    for n in range(2):
        rows_ref[n] = g1_ref[:, n * 128 : (n + 1) * 128]
    for q in range(4):
        dfield_ref[0:64, q * 256 : (q + 1) * 256] = g0[q * 64 : (q + 1) * 64, :]
        for n in range(2):
            at = slice(q * 256 + n * 128, q * 256 + (n + 1) * 128)
            dfield_ref[64:128, at] = rows_ref[n, pl.ds(q, 64, stride=4), :].astype(bf16)
    d_field = dfield_ref[...]
    own = core_ref[0]
    for out, part in ((keep_ref, own), (send_ref, 1 - own)):
        lhs = jnp.concatenate(
            [xnt_ref[pl.ds(pl.multiple_of(i * 64 + part * 32, 32), 32), :] for i in range(16)], axis=0
        )
        out[...] = dot(lhs, d_field).astype(bf16)


def render(core, latents, weight, gain, head, recv):
    slots = recv.shape[0]
    rays = 2 * slots
    blocks, wide = 64 // step_block, step_block * rays
    fold = fold_matrix()
    vmem = pl.BlockSpec(memory_space=pltpu.VMEM)
    return pl.pallas_call(
        render_kernel,
        out_shape=(
            jax.ShapeDtypeStruct((slots, 128), f32),
            jax.ShapeDtypeStruct(latents.shape, bf16),
            jax.ShapeDtypeStruct((512, 1024), bf16),
            jax.ShapeDtypeStruct((512, 1024), bf16),
        ),
        in_specs=[pl.BlockSpec(memory_space=pltpu.SMEM)] + [vmem] * 7,
        out_specs=(vmem,) * 4,
        scratch_shapes=[
            pltpu.VMEM((256, rays), f32),
            pltpu.VMEM((blocks, features, wide), bf16),
            pltpu.VMEM((blocks, 256, wide), bf16),
            pltpu.VMEM((blocks, 256, wide), bf16),
            pltpu.VMEM((2, 512, slots), f32),
            pltpu.VMEM((2, 512, slots), f32),
            pltpu.VMEM((features, 256), f32),
            pltpu.VMEM((256, 256), f32),
            pltpu.VMEM((2, 256, 128), f32),
            pltpu.VMEM((1024, 128), bf16),
        ],
        compiler_params=pltpu.CompilerParams(vmem_limit_bytes=48 * 1024 * 1024),
        cost_estimate=pl.CostEstimate(flops=12_000_000_000, bytes_accessed=8_000_000, transcendentals=1_000_000),
        name="render",
    )(core, latents, weight, gain, head, recv, jnp.asarray(fold, bf16), jnp.asarray(fold.T, bf16))


def latent_kernel(latent_ref, weight_ref, gain_ref, dfield_ref, out_ref):
    latent = latent_ref[...].astype(f32)
    inv_rms = lax.rsqrt(jnp.mean(latent * latent, axis=1, keepdims=True) + norm_eps)
    x_hat = latent * inv_rms
    d_scaled = dot(dfield_ref[...], weight_ref[...], (((1,), (1,)), ((), ()))) * gain_ref[...]
    mean = jnp.mean(d_scaled * x_hat, axis=1, keepdims=True)
    out_ref[...] = (inv_rms * (d_scaled - x_hat * mean)).astype(bf16)


def latent_gradient(latents, weight, gain, d_field):
    vmem = pl.BlockSpec(memory_space=pltpu.VMEM)
    return pl.pallas_call(
        latent_kernel,
        out_shape=jax.ShapeDtypeStruct(latents.shape, bf16),
        in_specs=[vmem] * 4,
        out_specs=vmem,
        compiler_params=pltpu.CompilerParams(vmem_limit_bytes=24 * 1024 * 1024),
        cost_estimate=pl.CostEstimate(flops=300_000_000, bytes_accessed=3_000_000, transcendentals=0),
        name="latent_gradient",
    )(latents, weight, gain, d_field)


def plane_kernel(terms_ref, weight_ref, gain_ref, sum_ref, gain_out_ref):
    total = terms_ref[0].astype(f32)
    for i in range(1, terms_ref.shape[0]):
        total = total + terms_ref[i].astype(f32)
    sum_ref[...] = total.astype(bf16)
    gain_part = jnp.sum(total * weight_ref[...].astype(f32), axis=1, keepdims=True) / gain_ref[...]
    line = jnp.concatenate([jnp.broadcast_to(gain_part, (32, 128)), jnp.zeros((96, 128), f32)], axis=0).T
    gain_out_ref[...] = line


def plane_sum(terms, weight_rows, gain_rows, slots):
    vmem = pl.BlockSpec(memory_space=pltpu.VMEM)
    return pl.pallas_call(
        plane_kernel,
        out_shape=(
            jax.ShapeDtypeStruct(weight_rows.shape, bf16),
            jax.ShapeDtypeStruct((slots, 128), f32),
        ),
        in_specs=[vmem] * 3,
        out_specs=(vmem,) * 2,
        cost_estimate=pl.CostEstimate(flops=1_000_000, bytes_accessed=1_300_000, transcendentals=0),
        name="plane_sum",
    )(terms, weight_rows, gain_rows)


def unpack_kernel(slot_ref, ret_ref, color_ref, loss_ref, rows_ref):
    rays = color_ref.shape[1]
    lane = lax.broadcasted_iota(jnp.int32, (1, 128), 1)
    for r in range(rays):
        slot = slot_ref[r]
        first = 3 * jnp.bitwise_and(slot, 1)
        kept = jnp.logical_and(lane >= first, lane < first + 3)
        rows_ref[r : r + 1, :] = jnp.where(kept, ret_ref[lax.shift_right_logical(slot, 1)], 0.0)
    turned = rows_ref[...].T
    color_ref[...] = turned[0:3, :] + turned[3:6, :]
    losses = jnp.where(lane == 6, jnp.sum(ret_ref[...], axis=0), 0.0)
    loss_ref[...] = jnp.sum(losses, axis=1, keepdims=True)


def unpack(slot, returned):
    vmem = pl.BlockSpec(memory_space=pltpu.VMEM)
    return pl.pallas_call(
        unpack_kernel,
        out_shape=(
            jax.ShapeDtypeStruct((3, slot.shape[0]), f32),
            jax.ShapeDtypeStruct((1, 1), f32),
        ),
        in_specs=[pl.BlockSpec(memory_space=pltpu.SMEM), vmem],
        out_specs=(vmem,) * 2,
        scratch_shapes=[pltpu.VMEM((slot.shape[0], 128), f32)],
        cost_estimate=pl.CostEstimate(flops=100_000, bytes_accessed=100_000, transcendentals=0),
        name="unpack",
    )(slot, returned)


def body(
    latents,
    head_weight,
    norm_gain,
    color_head,
    sample_points,
    sample_spacing,
    ray_targets,
    ray_scene,
):
    slots = lax.axis_size(both)
    shards = lax.axis_size("shard")
    groups = lax.axis_size("grp")
    shard = lax.axis_index("shard")
    gain_line = norm_gain[None, :]
    weight = lax.all_gather(head_weight, "shard", axis=0, tiled=True)
    sent, slot = pack(ray_scene, sample_points, sample_spacing, ray_targets, slots)
    recv = lax.all_to_all(sent, both, split_axis=0, concat_axis=0, tiled=True).reshape(slots, 640)
    core = (shard % 2).reshape(1).astype(jnp.int32)
    slot_colors, d_field, keep, send = render(core, latents, weight, gain_line, color_head, recv)

    other = lax.ppermute(send, "shard", [(i, i ^ 1) for i in range(shards)])
    paired = (keep.astype(f32) + other.astype(f32)).astype(bf16).reshape(shards // 2, shards, 1024)
    returned = lax.all_to_all(slot_colors.reshape(slots, 1, 128), both, split_axis=0, concat_axis=0, tiled=True)
    same_core = [[i for i in range(shards) if i % 2 == c] for c in range(2)]
    terms = lax.all_to_all(
        paired, "shard", split_axis=0, concat_axis=0, tiled=True, axis_index_groups=same_core
    )
    rendered, loss = unpack(slot, returned)
    latent_grad = latent_gradient(latents, weight, gain_line, d_field)
    gain_rows = lax.dynamic_slice(norm_gain, (shard * shards,), (shards,))[:, None]
    plane, gain_lines = plane_sum(terms, head_weight, gain_rows, slots)
    turns = [
        lax.ppermute(plane, "grp", [(i, (i + k) % groups) for i in range(groups)]).astype(f32)
        for k in range(1, groups)
    ]
    head_grad = (plane.astype(f32) + turns[1]) + (turns[0] + turns[2])
    gains = lax.all_to_all(gain_lines, both, split_axis=0, concat_axis=0, tiled=True)
    norm_gain_grad = jnp.sum(gains[:, :shards].reshape(groups, shards, shards), axis=0).reshape(-1)
    return (rendered, loss.reshape(()), head_grad, norm_gain_grad, latent_grad)


def solution(mesh):
    placed = (
        P(both, None),
        P("shard", None),
        P(),
        P(),
        P(both, None),
        P(both, None),
        P(None, both),
        P(both),
    )
    return jax.shard_map(
        body,
        mesh=mesh,
        in_specs=placed,
        out_specs=(
            P(None, both),
            P(),
            P("shard", None),
            P(),
            P(both, None),
        ),
        check_vma=False,
    )
```

```python
import jax
import jax.numpy as jnp
from jax import lax
from jax.experimental import pallas as pl
from jax.experimental.pallas import tpu as pltpu
from jax.sharding import PartitionSpec as P

norm_eps = 1e-06
f32, bf16 = jnp.float32, jnp.bfloat16
both = ("grp", "shard")

sin_coef = (3.141590256747904, -5.167405766362, 2.544000216186916, -0.5594350008327638)
cos_coef = (0.999999953027512, -4.934792802489427, 4.058410790762133, -1.3318729727851486, 0.21968242357146)

step_block = 8
features = 48


def fold_matrix():
    m = lax.broadcasted_iota(jnp.int32, (features, 256), 0).astype(f32)
    i = lax.broadcasted_iota(jnp.int32, (features, 256), 1).astype(f32)
    q = jnp.floor(i * (1 / 64) + 1 / 128)
    j = 4.0 * (i - 64.0 * q) + q
    jm = j - features * jnp.floor((j + 0.5) * (1 / features))
    coordinate = jnp.floor((m + 0.5) * (1 / 16))
    phase = jnp.floor((m - 16.0 * coordinate + 0.5) * (1 / 8))
    octave = m - 16.0 * coordinate - 8.0 * phase
    return (jm == coordinate + 3.0 * phase + 6.0 * octave).astype(f32)


def dot(a, b, dims=(((1,), (0,)), ((), ())), precision=None):
    return lax.dot_general(a, b, dims, preferred_element_type=f32, precision=precision)


def pack_kernel(scene_ref, points_ref, spacing_ref, target_ref, out_ref, slot_ref, count_ref, pay_ref, tint_ref):
    rays = points_ref.shape[0]
    for d in range(count_ref.shape[0]):
        count_ref[d] = 0
    out_ref[...] = jnp.zeros_like(out_ref)
    pay_ref[:, 0:192] = points_ref[...]
    pay_ref[:, 192:256] = spacing_ref[...]
    target = jnp.concatenate([target_ref[...], jnp.zeros((5, rays), f32)], axis=0).T
    lane = lax.broadcasted_iota(jnp.int32, (rays, 128), 1)
    for k in range(2):
        placed = jnp.zeros((rays, 128), f32)
        for c in range(3):
            placed = jnp.where(lane == 3 * k + c, target[:, c : c + 1], placed)
        tint_ref[k] = placed

    for r in range(rays):
        scene = scene_ref[r]
        rank = count_ref[scene]
        count_ref[scene] = rank + 1
        slot_ref[r] = scene * 2 + rank
        out_ref[scene, :, pl.ds(pl.multiple_of(rank * 256, 256), 256)] = pay_ref[r : r + 1, :]
        out_ref[scene, :, 512:640] += tint_ref[rank, r : r + 1, :]


def pack(ray_scene, points, spacing, targets, slots):
    rays = points.shape[0]
    return pl.pallas_call(
        pack_kernel,
        out_shape=(
            jax.ShapeDtypeStruct((slots, 1, 640), f32),
            jax.ShapeDtypeStruct((rays,), jnp.int32),
        ),
        in_specs=[pl.BlockSpec(memory_space=pltpu.SMEM)] + [pl.BlockSpec(memory_space=pltpu.VMEM)] * 3,
        out_specs=(pl.BlockSpec(memory_space=pltpu.VMEM), pl.BlockSpec(memory_space=pltpu.SMEM)),
        scratch_shapes=[
            pltpu.SMEM((slots,), jnp.int32),
            pltpu.VMEM((rays, 256), f32),
            pltpu.VMEM((2, rays, 128), f32),
        ],
        cost_estimate=pl.CostEstimate(flops=200000, bytes_accessed=1000000, transcendentals=0),
        name="pack",
    )(ray_scene, points, spacing, targets)


def field_kernel(
    core_ref,
    latent_ref,
    own_ref,
    other_ref,
    gain_ref,
    weight_ref,
    w0t_ref,
    w1_ref,
    w1t_ref,
    keep_ref,
    send_ref,
    rows_ref,
    turned_ref,
):
    scale = 1.0 / 16.0
    own = core_ref[0]
    for i in range(16):
        for part, ref in ((own, own_ref), (1 - own, other_ref)):
            weight_ref[pl.ds(pl.multiple_of(i * 64 + part * 32, 32), 32), :] = ref[i * 32 : (i + 1) * 32, :]
    latent = latent_ref[...].astype(f32)
    inv_rms = lax.rsqrt(jnp.mean(latent * latent, axis=1, keepdims=True) + norm_eps)
    normed = latent * inv_rms * gain_ref[...]
    field = dot(normed.astype(bf16), weight_ref[...]).astype(bf16)
    stacked = jnp.concatenate([field[0:64, q * 256 : (q + 1) * 256] for q in range(4)], axis=0)
    folded = dot(fold_matrix().astype(bf16), stacked) * scale
    high = folded.astype(bf16).astype(f32)
    split = jnp.concatenate([high, folded - high, jnp.zeros((32, 256), f32)], axis=0)
    w0t_ref[...] = split.T.astype(bf16)
    field1 = field[64:128, :].astype(f32) * scale
    for q in range(4):
        for n in range(2):
            rows_ref[n, pl.ds(q, 64, stride=4), :] = field1[:, q * 256 + n * 128 : q * 256 + (n + 1) * 128]
    w1f = jnp.concatenate([rows_ref[0], rows_ref[1]], axis=1)
    w1_ref[...] = w1f.astype(bf16)
    w1t_ref[...] = w1f.T.astype(bf16)
    turned_ref[...] = normed.T.astype(bf16)
    for out, part in ((keep_ref, own), (send_ref, 1 - own)):
        for i in range(16):
            out[i * 32 : (i + 1) * 32, :] = turned_ref[pl.ds(pl.multiple_of(i * 64 + part * 32, 32), 32), :]


def make_field(core, latents, own_rows, other_rows, gain):
    vmem = pl.BlockSpec(memory_space=pltpu.VMEM)
    shapes = ((1024, 1024), (256, 128), (256, 256), (256, 256), (512, 128), (512, 128))
    return pl.pallas_call(
        field_kernel,
        out_shape=tuple(jax.ShapeDtypeStruct(shape, bf16) for shape in shapes),
        in_specs=[pl.BlockSpec(memory_space=pltpu.SMEM)] + [vmem] * 4,
        out_specs=(vmem,) * 6,
        scratch_shapes=[pltpu.VMEM((2, 256, 128), f32), pltpu.VMEM((1024, 128), bf16)],
        compiler_params=pltpu.CompilerParams(vmem_limit_bytes=24 * 1024 * 1024),
        cost_estimate=pl.CostEstimate(flops=400_000_000, bytes_accessed=5_000_000, transcendentals=0),
        name="field",
    )(core, latents, own_rows, other_rows, gain)


def horner(u, coef):
    value = coef[-1] * u + coef[-2]
    for c in coef[-3::-1]:
        value = value * u + c
    return value


def render_kernel(
    recv_ref,
    w0t_ref,
    w1_ref,
    w1t_ref,
    head_ref,
    color_ref,
    dfield_ref,
    rays_ref,
    h0_ref,
    h1_ref,
    h2_ref,
    raw_ref,
    draw_ref,
    g0_ref,
    g1_ref,
    rows_ref,
):
    scale = 1.0 / 16.0
    slots = recv_ref.shape[0]
    rays = 2 * slots
    blocks = 64 // step_block

    for k in range(2):
        rays_ref[0:256, k * slots : (k + 1) * slots] = recv_ref[:, k * 256 : (k + 1) * 256].T
    tint = recv_ref[:, 512:640].T
    w0t = w0t_ref[:, 0:96]
    w1 = w1_ref[...]
    w1t = w1t_ref[...]
    head_f = jnp.concatenate([head_ref[...].astype(f32), jnp.zeros((4, 256), f32)], axis=0)
    head = head_f.astype(bf16)
    head_t = (head_f * scale).T.astype(bf16)

    octave = jnp.left_shift(1, lax.broadcasted_iota(jnp.int32, (8, rays), 0)).astype(f32)

    def forward(b, carry):
        parts = [[] for _ in range(6)]
        for c in range(3):
            group = rays_ref[pl.ds(pl.multiple_of(c * 64 + b * step_block, 8), step_block), :]
            for s in range(step_block):
                y = group[s : s + 1, :] * octave
                whole = jnp.floor(y + 0.5)
                r = y - whole
                half = whole * 0.5
                sign = 1.0 - 4.0 * (half - jnp.floor(half))
                u = r * r
                parts[2 * c].append(r * sign * horner(u, sin_coef))
                parts[2 * c + 1].append(sign * horner(u, cos_coef))
        h0 = jnp.concatenate([jnp.concatenate(p, axis=1) for p in parts], axis=0).astype(bf16)
        h0_ref[b] = h0
        h1 = jnp.maximum(dot(w0t, jnp.concatenate([h0, h0], axis=0)), 0.0).astype(bf16)
        h1_ref[b] = h1
        h2 = jnp.maximum(dot(w1t, h1), 0.0).astype(bf16)
        h2_ref[b] = h2
        raw = dot(head, h2)
        for s in range(step_block):
            at = pl.ds(pl.multiple_of((b * step_block + s) * 8, 8), 8)
            for k in range(2):
                raw_ref[k, at, :] = raw[:, (2 * s + k) * slots : (2 * s + k + 1) * slots]
        return carry

    lax.fori_loop(0, blocks, forward, 0)

    def spread(c):
        return jnp.concatenate([raw_ref[k, pl.ds(c, 64, stride=8), :] for k in range(2)], axis=1)

    def store_gradient(c, value):
        for k in range(2):
            draw_ref[k, pl.ds(c, 64, stride=8), :] = value[:, k * slots : (k + 1) * slots]

    spacing = rays_ref[192:256, :]
    row = lax.broadcasted_iota(jnp.int32, (64, 64), 0)
    column = lax.broadcasted_iota(jnp.int32, (64, 64), 1)
    raw0 = spread(0)
    density = jnp.maximum(raw0, 0.0) + jnp.log1p(jnp.exp(-jnp.abs(raw0)))
    optical = density * spacing
    before = dot((column < row).astype(f32), optical, precision=lax.Precision.HIGHEST)
    transmit = jnp.exp(-before)
    survive = jnp.exp(-optical)
    blend = transmit * (1.0 - survive)
    live = (spacing[0:1, :] > 0.0).astype(f32)
    factor = 1.0 / (float(slots) * jnp.sum(live, axis=1, keepdims=True))
    albedo = [jax.nn.sigmoid(spread(1 + c)) for c in range(3)]
    d_blend = jnp.zeros_like(blend)
    square = jnp.zeros_like(live)
    colors, grads = [], []
    for c in range(3):
        color = jnp.sum(blend * (albedo[c] - 1.0), axis=0, keepdims=True) + 1.0
        target = jnp.concatenate([tint[c : c + 1, :], tint[3 + c : 4 + c, :]], axis=1)
        residual = (color - target) * live
        square = square + residual * residual
        grad = 2.0 * residual * factor
        d_blend = d_blend + grad * (albedo[c] - 1.0)
        colors.append(color)
        grads.append(grad)
    loss = jnp.sum(square, axis=1, keepdims=True) * factor
    rows = [colors[c][:, k * slots : (k + 1) * slots] for k in range(2) for c in range(3)]
    rows = [jnp.zeros((40, slots), f32), *rows, jnp.broadcast_to(loss, (1, slots))]
    color_ref[...] = jnp.concatenate([*rows, jnp.zeros((slots - 47, slots), f32)], axis=0).T
    weighted = d_blend * blend
    behind = dot((column > row).astype(f32), weighted, precision=lax.Precision.HIGHEST)
    d_optical = d_blend * transmit * survive - behind
    draw_ref[...] = jnp.zeros_like(draw_ref)
    store_gradient(0, d_optical * spacing * jax.nn.sigmoid(raw0))
    for c in range(3):
        store_gradient(1 + c, grads[c] * blend * albedo[c] * (1.0 - albedo[c]))

    g0_ref[...] = jnp.zeros_like(g0_ref)
    g1_ref[...] = jnp.zeros_like(g1_ref)
    on_lanes = (((1,), (1,)), ((), ()))

    def backward(b, carry):
        d_raw = jnp.concatenate(
            [
                draw_ref[k, pl.ds(pl.multiple_of((b * step_block + s) * 8, 8), 8), :]
                for s in range(step_block)
                for k in range(2)
            ],
            axis=1,
        ).astype(bf16)
        h1 = h1_ref[b]
        d_a2 = jnp.where(h2_ref[b] > 0, dot(head_t, d_raw).astype(bf16), jnp.zeros((), bf16))
        d_a1 = jnp.where(h1 > 0, dot(w1, d_a2).astype(bf16), jnp.zeros((), bf16))
        g1_ref[...] += dot(h1, d_a2, on_lanes)
        g0_ref[...] += dot(h0_ref[b], d_a1, on_lanes)
        return carry

    lax.fori_loop(0, blocks, backward, 0)

    unfold = jnp.concatenate([fold_matrix(), jnp.zeros((80, 256), f32)], axis=0).T[:, 0:features].astype(bf16)
    g0 = dot(unfold, g0_ref[...].astype(bf16)).astype(bf16)
    for n in range(2):
        rows_ref[n] = g1_ref[:, n * 128 : (n + 1) * 128]
    for q in range(4):
        dfield_ref[0:64, q * 256 : (q + 1) * 256] = g0[q * 64 : (q + 1) * 64, :]
        for n in range(2):
            at = slice(q * 256 + n * 128, q * 256 + (n + 1) * 128)
            dfield_ref[64:128, at] = rows_ref[n, pl.ds(q, 64, stride=4), :].astype(bf16)


def render(recv, w0t, w1, w1t, head):
    slots = recv.shape[0]
    rays = 2 * slots
    blocks, wide = 64 // step_block, step_block * rays
    vmem = pl.BlockSpec(memory_space=pltpu.VMEM)
    return pl.pallas_call(
        render_kernel,
        out_shape=(
            jax.ShapeDtypeStruct((slots, 128), f32),
            jax.ShapeDtypeStruct((128, 1024), bf16),
        ),
        in_specs=[vmem] * 5,
        out_specs=(vmem,) * 2,
        scratch_shapes=[
            pltpu.VMEM((256, rays), f32),
            pltpu.VMEM((blocks, features, wide), bf16),
            pltpu.VMEM((blocks, 256, wide), bf16),
            pltpu.VMEM((blocks, 256, wide), bf16),
            pltpu.VMEM((2, 512, slots), f32),
            pltpu.VMEM((2, 512, slots), f32),
            pltpu.VMEM((features, 256), f32),
            pltpu.VMEM((256, 256), f32),
            pltpu.VMEM((2, 256, 128), f32),
        ],
        compiler_params=pltpu.CompilerParams(vmem_limit_bytes=44 * 1024 * 1024),
        cost_estimate=pl.CostEstimate(flops=12_000_000_000, bytes_accessed=2_000_000, transcendentals=1_000_000),
        name="render",
    )(recv, w0t, w1, w1t, head)


def pair_kernel(keep_ref, other_ref, dfield_ref, dother_ref, out_ref):
    out_ref[...] = (dot(keep_ref[...], dfield_ref[...]) + dot(other_ref[...], dother_ref[...])).astype(bf16)


def pair_terms(keep, other, d_field, d_other):
    vmem = pl.BlockSpec(memory_space=pltpu.VMEM)
    return pl.pallas_call(
        pair_kernel,
        out_shape=jax.ShapeDtypeStruct((512, 1024), bf16),
        in_specs=[vmem] * 4,
        out_specs=vmem,
        compiler_params=pltpu.CompilerParams(vmem_limit_bytes=16 * 1024 * 1024),
        cost_estimate=pl.CostEstimate(flops=270_000_000, bytes_accessed=2_000_000, transcendentals=0),
        name="pair_terms",
    )(keep, other, d_field, d_other)


def latent_kernel(latent_ref, weight_ref, gain_ref, dfield_ref, out_ref):
    latent = latent_ref[...].astype(f32)
    inv_rms = lax.rsqrt(jnp.mean(latent * latent, axis=1, keepdims=True) + norm_eps)
    x_hat = latent * inv_rms
    d_scaled = dot(dfield_ref[...], weight_ref[...], (((1,), (1,)), ((), ()))) * gain_ref[...]
    mean = jnp.mean(d_scaled * x_hat, axis=1, keepdims=True)
    out_ref[...] = (inv_rms * (d_scaled - x_hat * mean)).astype(bf16)


def latent_gradient(latents, weight, gain, d_field):
    vmem = pl.BlockSpec(memory_space=pltpu.VMEM)
    return pl.pallas_call(
        latent_kernel,
        out_shape=jax.ShapeDtypeStruct(latents.shape, bf16),
        in_specs=[vmem] * 4,
        out_specs=vmem,
        compiler_params=pltpu.CompilerParams(vmem_limit_bytes=24 * 1024 * 1024),
        cost_estimate=pl.CostEstimate(flops=300_000_000, bytes_accessed=3_000_000, transcendentals=0),
        name="latent_gradient",
    )(latents, weight, gain, d_field)


def plane_kernel(terms_ref, weight_ref, color_ref, sum_ref, line_ref):
    total = terms_ref[0].astype(f32)
    for i in range(1, terms_ref.shape[0]):
        total = total + terms_ref[i].astype(f32)
    sum_ref[...] = total.astype(bf16)
    part = jnp.sum(total * weight_ref[...].astype(f32), axis=1, keepdims=True)
    line = jnp.concatenate([jnp.broadcast_to(part, (32, 128)), jnp.zeros((96, 128), f32)], axis=0).T
    line_ref[...] = line + color_ref[...]


def plane_sum(terms, weight_rows, colors):
    vmem = pl.BlockSpec(memory_space=pltpu.VMEM)
    return pl.pallas_call(
        plane_kernel,
        out_shape=(
            jax.ShapeDtypeStruct(weight_rows.shape, bf16),
            jax.ShapeDtypeStruct(colors.shape, f32),
        ),
        in_specs=[vmem] * 3,
        out_specs=(vmem,) * 2,
        cost_estimate=pl.CostEstimate(flops=1_000_000, bytes_accessed=1_300_000, transcendentals=0),
        name="plane_sum",
    )(terms, weight_rows, colors)


def unpack_kernel(slot_ref, ret_ref, gain_ref, color_ref, loss_ref, gain_out_ref, rows_ref):
    rays = color_ref.shape[1]
    lane = lax.broadcasted_iota(jnp.int32, (1, 128), 1)
    total = ret_ref[0:32, 0, :]
    for z in range(1, 4):
        total = total + ret_ref[z * 32 : (z + 1) * 32, 0, :]
    rows_ref[0:32, :] = total
    gains = [rows_ref[pl.ds(i, 8, stride=4), :][:, 0:32] for i in range(4)]
    gain_out_ref[...] = jnp.concatenate(gains, axis=1) / gain_ref[...]
    for r in range(rays):
        slot = slot_ref[r]
        first = 40 + 3 * jnp.bitwise_and(slot, 1)
        kept = jnp.logical_and(lane >= first, lane < first + 3)
        rows_ref[r : r + 1, :] = jnp.where(kept, ret_ref[lax.shift_right_logical(slot, 1)], 0.0)
    turned = rows_ref[...].T
    color_ref[...] = turned[40:43, :] + turned[43:46, :]
    losses = jnp.where(lane == 46, jnp.sum(ret_ref[...], axis=0), 0.0)
    loss_ref[...] = jnp.sum(losses, axis=1, keepdims=True)


def unpack(slot, returned, gain):
    vmem = pl.BlockSpec(memory_space=pltpu.VMEM)
    return pl.pallas_call(
        unpack_kernel,
        out_shape=(
            jax.ShapeDtypeStruct((3, slot.shape[0]), f32),
            jax.ShapeDtypeStruct((1, 1), f32),
            jax.ShapeDtypeStruct(gain.shape, f32),
        ),
        in_specs=[pl.BlockSpec(memory_space=pltpu.SMEM), vmem, vmem],
        out_specs=(vmem,) * 3,
        scratch_shapes=[pltpu.VMEM((slot.shape[0], 128), f32)],
        cost_estimate=pl.CostEstimate(flops=100_000, bytes_accessed=100_000, transcendentals=0),
        name="unpack",
    )(slot, returned, gain)


def body(
    latents,
    head_weight,
    norm_gain,
    color_head,
    sample_points,
    sample_spacing,
    ray_targets,
    ray_scene,
):
    slots = lax.axis_size(both)
    shards = lax.axis_size("shard")
    groups = lax.axis_size("grp")
    core = (lax.axis_index("shard") % 2).reshape(1).astype(jnp.int32)
    gain_line = norm_gain[None, :]
    same_core = [[i for i in range(shards) if i % 2 == c] for c in range(2)]
    across = [(i, i ^ 1) for i in range(shards)]

    def among_same_core(x):
        return lax.all_to_all(x, "shard", split_axis=0, concat_axis=0, tiled=True, axis_index_groups=same_core)

    def among_all(x):
        return lax.all_to_all(x, both, split_axis=0, concat_axis=0, tiled=True)

    own_rows = among_same_core(jnp.broadcast_to(head_weight[None], (shards // 2, *head_weight.shape)))
    own_rows = own_rows.reshape(512, 1024)
    sent, slot = pack(ray_scene, sample_points, sample_spacing, ray_targets, slots)
    sent, own_rows = lax.optimization_barrier((sent, own_rows))
    other_rows = lax.ppermute(own_rows, "shard", across)
    recv = among_all(sent).reshape(slots, 640)
    weight, w0t, w1, w1t, keep, send = make_field(core, latents, own_rows, other_rows, gain_line)
    x_other = lax.ppermute(send, "shard", across)
    colors, d_field = render(recv, w0t, w1, w1t, color_head)
    d_other = lax.ppermute(d_field, "shard", across)
    paired = pair_terms(keep, x_other, d_field, d_other)
    terms = among_same_core(paired.reshape(shards // 2, shards, 1024))
    latent_grad = latent_gradient(latents, weight, gain_line, d_field)
    plane, lines = plane_sum(terms, head_weight, colors)
    turns = [
        lax.ppermute(plane, "grp", [(i, (i + k) % groups) for i in range(groups)]).astype(f32)
        for k in range(1, groups)
    ]
    head_grad = (plane.astype(f32) + turns[1]) + (turns[0] + turns[2])
    returned = among_all(lines.reshape(slots, 1, 128))
    rendered, loss, gain_grad = unpack(slot, returned, norm_gain.reshape(8, 128))
    return (rendered, loss.reshape(()), head_grad, gain_grad.reshape(-1), latent_grad)


def solution(mesh):
    placed = (
        P(both, None),
        P("shard", None),
        P(),
        P(),
        P(both, None),
        P(both, None),
        P(None, both),
        P(both),
    )
    return jax.shard_map(
        body,
        mesh=mesh,
        in_specs=placed,
        out_specs=(
            P(None, both),
            P(),
            P("shard", None),
            P(),
            P(both, None),
        ),
        check_vma=False,
    )
```

```python
import jax
import jax.numpy as jnp
from jax import lax
from jax.experimental import pallas as pl
from jax.experimental.pallas import tpu as pltpu
from jax.sharding import PartitionSpec as P

norm_eps = 1e-06
f32, bf16 = jnp.float32, jnp.bfloat16
both = ("grp", "shard")

sin_coef = (3.141590256747904, -5.167405766362, 2.544000216186916, -0.5594350008327638)
cos_coef = (0.999999953027512, -4.934792802489427, 4.058410790762133, -1.3318729727851486, 0.21968242357146)

step_block = 8
features = 48


def fold_matrix():
    m = lax.broadcasted_iota(jnp.int32, (features, 256), 0).astype(f32)
    i = lax.broadcasted_iota(jnp.int32, (features, 256), 1).astype(f32)
    q = jnp.floor(i * (1 / 64) + 1 / 128)
    j = 4.0 * (i - 64.0 * q) + q
    jm = j - features * jnp.floor((j + 0.5) * (1 / features))
    coordinate = jnp.floor((m + 0.5) * (1 / 16))
    phase = jnp.floor((m - 16.0 * coordinate + 0.5) * (1 / 8))
    octave = m - 16.0 * coordinate - 8.0 * phase
    return (jm == coordinate + 3.0 * phase + 6.0 * octave).astype(f32)


def dot(a, b, dims=(((1,), (0,)), ((), ())), precision=None):
    return lax.dot_general(a, b, dims, preferred_element_type=f32, precision=precision)


def pack_kernel(scene_ref, points_ref, spacing_ref, target_ref, out_ref, slot_ref, count_ref, pay_ref, tint_ref):
    rays = points_ref.shape[0]
    for d in range(count_ref.shape[0]):
        count_ref[d] = 0
    out_ref[...] = jnp.zeros_like(out_ref)
    pay_ref[:, 0:192] = points_ref[...]
    pay_ref[:, 192:256] = spacing_ref[...]
    target = jnp.concatenate([target_ref[...], jnp.zeros((5, rays), f32)], axis=0).T
    lane = lax.broadcasted_iota(jnp.int32, (rays, 128), 1)
    for k in range(2):
        placed = jnp.zeros((rays, 128), f32)
        for c in range(3):
            placed = jnp.where(lane == 3 * k + c, target[:, c : c + 1], placed)
        tint_ref[k] = placed

    for r in range(rays):
        scene = scene_ref[r]
        rank = count_ref[scene]
        count_ref[scene] = rank + 1
        slot_ref[r] = scene * 2 + rank
        out_ref[scene, :, pl.ds(pl.multiple_of(rank * 256, 256), 256)] = pay_ref[r : r + 1, :]
        out_ref[scene, :, 512:640] += tint_ref[rank, r : r + 1, :]


def pack(ray_scene, points, spacing, targets, slots):
    rays = points.shape[0]
    return pl.pallas_call(
        pack_kernel,
        out_shape=(
            jax.ShapeDtypeStruct((slots, 1, 640), f32),
            jax.ShapeDtypeStruct((rays,), jnp.int32),
        ),
        in_specs=[pl.BlockSpec(memory_space=pltpu.SMEM)] + [pl.BlockSpec(memory_space=pltpu.VMEM)] * 3,
        out_specs=(pl.BlockSpec(memory_space=pltpu.VMEM), pl.BlockSpec(memory_space=pltpu.SMEM)),
        scratch_shapes=[
            pltpu.SMEM((slots,), jnp.int32),
            pltpu.VMEM((rays, 256), f32),
            pltpu.VMEM((2, rays, 128), f32),
        ],
        cost_estimate=pl.CostEstimate(flops=200000, bytes_accessed=1000000, transcendentals=0),
        name="pack",
    )(ray_scene, points, spacing, targets)


def field_kernel(
    core_ref,
    latent_ref,
    own_ref,
    other_ref,
    gain_ref,
    weight_ref,
    w0t_ref,
    w1_ref,
    w1t_ref,
    keep_ref,
    send_ref,
    rows_ref,
    turned_ref,
):
    scale = 1.0 / 16.0
    own = core_ref[0]
    for i in range(16):
        for part, ref in ((own, own_ref), (1 - own, other_ref)):
            weight_ref[pl.ds(pl.multiple_of(i * 64 + part * 32, 32), 32), :] = ref[i * 32 : (i + 1) * 32, :]
    latent = latent_ref[...].astype(f32)
    inv_rms = lax.rsqrt(jnp.mean(latent * latent, axis=1, keepdims=True) + norm_eps)
    normed = latent * inv_rms * gain_ref[...]
    field = dot(normed.astype(bf16), weight_ref[...]).astype(bf16)
    stacked = jnp.concatenate([field[0:64, q * 256 : (q + 1) * 256] for q in range(4)], axis=0)
    folded = dot(fold_matrix().astype(bf16), stacked) * scale
    high = folded.astype(bf16).astype(f32)
    split = jnp.concatenate([high, folded - high, jnp.zeros((32, 256), f32)], axis=0)
    w0t_ref[...] = split.T.astype(bf16)
    field1 = field[64:128, :].astype(f32) * scale
    for q in range(4):
        for n in range(2):
            rows_ref[n, pl.ds(q, 64, stride=4), :] = field1[:, q * 256 + n * 128 : q * 256 + (n + 1) * 128]
    w1f = jnp.concatenate([rows_ref[0], rows_ref[1]], axis=1)
    w1_ref[...] = w1f.astype(bf16)
    w1t_ref[...] = w1f.T.astype(bf16)
    turned_ref[...] = normed.T.astype(bf16)
    for out, part in ((keep_ref, own), (send_ref, 1 - own)):
        for i in range(16):
            out[i * 32 : (i + 1) * 32, :] = turned_ref[pl.ds(pl.multiple_of(i * 64 + part * 32, 32), 32), :]


def make_field(core, latents, own_rows, other_rows, gain):
    vmem = pl.BlockSpec(memory_space=pltpu.VMEM)
    shapes = ((1024, 1024), (256, 128), (256, 256), (256, 256), (512, 128), (512, 128))
    return pl.pallas_call(
        field_kernel,
        out_shape=tuple(jax.ShapeDtypeStruct(shape, bf16) for shape in shapes),
        in_specs=[pl.BlockSpec(memory_space=pltpu.SMEM)] + [vmem] * 4,
        out_specs=(vmem,) * 6,
        scratch_shapes=[pltpu.VMEM((2, 256, 128), f32), pltpu.VMEM((1024, 128), bf16)],
        compiler_params=pltpu.CompilerParams(vmem_limit_bytes=24 * 1024 * 1024),
        cost_estimate=pl.CostEstimate(flops=400_000_000, bytes_accessed=5_000_000, transcendentals=0),
        name="field",
    )(core, latents, own_rows, other_rows, gain)


def horner(u, coef):
    value = coef[-1] * u + coef[-2]
    for c in coef[-3::-1]:
        value = value * u + c
    return value


def render_kernel(
    recv_ref,
    w0t_ref,
    w1_ref,
    w1t_ref,
    head_ref,
    color_ref,
    dfield_ref,
    rays_ref,
    h0_ref,
    h1_ref,
    h2_ref,
    raw_ref,
    draw_ref,
    g0_ref,
    g1_ref,
    rows_ref,
):
    scale = 1.0 / 16.0
    slots = recv_ref.shape[0]
    rays = 2 * slots
    blocks = 64 // step_block

    for k in range(2):
        rays_ref[0:256, k * slots : (k + 1) * slots] = recv_ref[:, k * 256 : (k + 1) * 256].T
    tint = recv_ref[:, 512:640].T
    w0t = w0t_ref[:, 0:96]
    w1 = w1_ref[...]
    w1t = w1t_ref[...]
    head_f = jnp.concatenate([head_ref[...].astype(f32), jnp.zeros((4, 256), f32)], axis=0)
    head = head_f.astype(bf16)
    head_t = (head_f * scale).T.astype(bf16)

    octave = jnp.left_shift(1, lax.broadcasted_iota(jnp.int32, (8, rays), 0)).astype(f32)

    def forward(b, carry):
        parts = [[] for _ in range(6)]
        for c in range(3):
            group = rays_ref[pl.ds(pl.multiple_of(c * 64 + b * step_block, 8), step_block), :]
            for s in range(step_block):
                y = group[s : s + 1, :] * octave
                whole = jnp.floor(y + 0.5)
                r = y - whole
                half = whole * 0.5
                sign = 1.0 - 4.0 * (half - jnp.floor(half))
                u = r * r
                parts[2 * c].append(r * sign * horner(u, sin_coef))
                parts[2 * c + 1].append(sign * horner(u, cos_coef))
        h0 = jnp.concatenate([jnp.concatenate(p, axis=1) for p in parts], axis=0).astype(bf16)
        h0_ref[b] = h0
        h1 = jnp.maximum(dot(w0t, jnp.concatenate([h0, h0], axis=0)), 0.0).astype(bf16)
        h1_ref[b] = h1
        h2 = jnp.maximum(dot(w1t, h1), 0.0).astype(bf16)
        h2_ref[b] = h2
        raw = dot(head, h2)
        for s in range(step_block):
            at = pl.ds(pl.multiple_of((b * step_block + s) * 8, 8), 8)
            for k in range(2):
                raw_ref[k, at, :] = raw[:, (2 * s + k) * slots : (2 * s + k + 1) * slots]
        return carry

    lax.fori_loop(0, blocks, forward, 0, unroll=True)

    def spread(c):
        return jnp.concatenate([raw_ref[k, pl.ds(c, 64, stride=8), :] for k in range(2)], axis=1)

    def store_gradient(c, value):
        for k in range(2):
            draw_ref[k, pl.ds(c, 64, stride=8), :] = value[:, k * slots : (k + 1) * slots]

    spacing = rays_ref[192:256, :]
    row = lax.broadcasted_iota(jnp.int32, (64, 64), 0)
    column = lax.broadcasted_iota(jnp.int32, (64, 64), 1)
    raw0 = spread(0)
    density = jnp.maximum(raw0, 0.0) + jnp.log1p(jnp.exp(-jnp.abs(raw0)))
    optical = density * spacing
    before = dot((column < row).astype(f32), optical, precision=lax.Precision.HIGHEST)
    transmit = jnp.exp(-before)
    survive = jnp.exp(-optical)
    blend = transmit * (1.0 - survive)
    live = (spacing[0:1, :] > 0.0).astype(f32)
    factor = 1.0 / (float(slots) * jnp.sum(live, axis=1, keepdims=True))
    albedo = [jax.nn.sigmoid(spread(1 + c)) for c in range(3)]
    d_blend = jnp.zeros_like(blend)
    square = jnp.zeros_like(live)
    colors, grads = [], []
    for c in range(3):
        color = jnp.sum(blend * (albedo[c] - 1.0), axis=0, keepdims=True) + 1.0
        target = jnp.concatenate([tint[c : c + 1, :], tint[3 + c : 4 + c, :]], axis=1)
        residual = (color - target) * live
        square = square + residual * residual
        grad = 2.0 * residual * factor
        d_blend = d_blend + grad * (albedo[c] - 1.0)
        colors.append(color)
        grads.append(grad)
    loss = jnp.sum(square, axis=1, keepdims=True) * factor
    rows = [colors[c][:, k * slots : (k + 1) * slots] for k in range(2) for c in range(3)]
    color_ref[...] = jnp.concatenate([*rows, jnp.broadcast_to(loss, (2, slots))], axis=0)
    weighted = d_blend * blend
    behind = dot((column > row).astype(f32), weighted, precision=lax.Precision.HIGHEST)
    d_optical = d_blend * transmit * survive - behind
    draw_ref[...] = jnp.zeros_like(draw_ref)
    store_gradient(0, d_optical * spacing * jax.nn.sigmoid(raw0))
    for c in range(3):
        store_gradient(1 + c, grads[c] * blend * albedo[c] * (1.0 - albedo[c]))

    g0_ref[...] = jnp.zeros_like(g0_ref)
    g1_ref[...] = jnp.zeros_like(g1_ref)
    on_lanes = (((1,), (1,)), ((), ()))

    def backward(b, carry):
        d_raw = jnp.concatenate(
            [
                draw_ref[k, pl.ds(pl.multiple_of((b * step_block + s) * 8, 8), 8), :]
                for s in range(step_block)
                for k in range(2)
            ],
            axis=1,
        ).astype(bf16)
        h1 = h1_ref[b]
        d_a2 = jnp.where(h2_ref[b] > 0, dot(head_t, d_raw).astype(bf16), jnp.zeros((), bf16))
        d_a1 = jnp.where(h1 > 0, dot(w1, d_a2).astype(bf16), jnp.zeros((), bf16))
        g1_ref[...] += dot(h1, d_a2, on_lanes)
        g0_ref[...] += dot(h0_ref[b], d_a1, on_lanes)
        return carry

    lax.fori_loop(0, blocks, backward, 0, unroll=True)

    unfold = jnp.concatenate([fold_matrix(), jnp.zeros((80, 256), f32)], axis=0).T[:, 0:features].astype(bf16)
    g0 = dot(unfold, g0_ref[...].astype(bf16)).astype(bf16)
    for n in range(2):
        rows_ref[n] = g1_ref[:, n * 128 : (n + 1) * 128]
    for q in range(4):
        dfield_ref[0:64, q * 256 : (q + 1) * 256] = g0[q * 64 : (q + 1) * 64, :]
        for n in range(2):
            at = slice(q * 256 + n * 128, q * 256 + (n + 1) * 128)
            dfield_ref[64:128, at] = rows_ref[n, pl.ds(q, 64, stride=4), :].astype(bf16)


def render(recv, w0t, w1, w1t, head):
    slots = recv.shape[0]
    rays = 2 * slots
    blocks, wide = 64 // step_block, step_block * rays
    vmem = pl.BlockSpec(memory_space=pltpu.VMEM)
    return pl.pallas_call(
        render_kernel,
        out_shape=(
            jax.ShapeDtypeStruct((8, slots), f32),
            jax.ShapeDtypeStruct((128, 1024), bf16),
        ),
        in_specs=[vmem] * 5,
        out_specs=(vmem,) * 2,
        scratch_shapes=[
            pltpu.VMEM((256, rays), f32),
            pltpu.VMEM((blocks, features, wide), bf16),
            pltpu.VMEM((blocks, 256, wide), bf16),
            pltpu.VMEM((blocks, 256, wide), bf16),
            pltpu.VMEM((2, 512, slots), f32),
            pltpu.VMEM((2, 512, slots), f32),
            pltpu.VMEM((features, 256), f32),
            pltpu.VMEM((256, 256), f32),
            pltpu.VMEM((2, 256, 128), f32),
        ],
        compiler_params=pltpu.CompilerParams(vmem_limit_bytes=44 * 1024 * 1024),
        cost_estimate=pl.CostEstimate(flops=12_000_000_000, bytes_accessed=2_000_000, transcendentals=1_000_000),
        name="render",
    )(recv, w0t, w1, w1t, head)


def latent_kernel(latent_ref, weight_ref, gain_ref, dfield_ref, color_ref, out_ref, note_ref):
    latent = latent_ref[...].astype(f32)
    inv_rms = lax.rsqrt(jnp.mean(latent * latent, axis=1, keepdims=True) + norm_eps)
    x_hat = latent * inv_rms
    d_norm = dot(dfield_ref[...], weight_ref[...], (((1,), (1,)), ((), ())))
    term = d_norm * x_hat
    gain = jnp.sum(term, axis=0, keepdims=True)
    mean = jnp.mean(term * gain_ref[...], axis=1, keepdims=True)
    out_ref[...] = (inv_rms * (d_norm * gain_ref[...] - x_hat * mean)).astype(bf16)
    note_ref[0:8, :] = color_ref[...]
    for i in range(8):
        note_ref[8 + i : 9 + i, :] = gain[:, i * 128 : (i + 1) * 128]


def latent_gradient(latents, weight, gain, d_field, colors):
    vmem = pl.BlockSpec(memory_space=pltpu.VMEM)
    return pl.pallas_call(
        latent_kernel,
        out_shape=(
            jax.ShapeDtypeStruct(latents.shape, bf16),
            jax.ShapeDtypeStruct((16, 128), f32),
        ),
        in_specs=[vmem] * 5,
        out_specs=(vmem,) * 2,
        compiler_params=pltpu.CompilerParams(vmem_limit_bytes=24 * 1024 * 1024),
        cost_estimate=pl.CostEstimate(flops=300_000_000, bytes_accessed=3_000_000, transcendentals=0),
        name="latent_gradient",
    )(latents, weight, gain, d_field, colors)


def two_terms(value):
    high = value.astype(bf16).astype(f32)
    return high, value - high


def pair_kernel(
    core_ref, keep_ref, other_ref, dfield_ref, dother_ref, note_ref, nother_ref, out_ref, turned_ref
):
    first = core_ref[0] == 0
    mine, mate = note_ref[...], nother_ref[...]
    colors = jnp.concatenate(
        [jnp.where(first, mine, mate)[0:8, :], jnp.where(first, mate, mine)[0:8, :], jnp.zeros((112, 128), f32)],
        axis=0,
    )
    turned_ref[...] = colors.T
    gain = two_terms(mine[8:16, :] + mate[8:16, :])
    terms = (dot(keep_ref[...], dfield_ref[...]) + dot(other_ref[...], dother_ref[...])).astype(bf16)
    for i in range(16):
        out_ref[i, :, 0:1024] = terms[i * 32 : (i + 1) * 32, :]
        rows = [turned_ref[pl.ds(2 * i + c, 4, stride=32), :] for c in range(2)]
        tint = two_terms(jnp.where(first, *rows))
        out_ref[i, :, 1024:1152] = jnp.concatenate(
            [*tint, *gain, jnp.zeros((8, 128), f32)], axis=0
        ).astype(bf16)


def pair_terms(core, keep, other, d_field, d_other, note, note_other):
    vmem = pl.BlockSpec(memory_space=pltpu.VMEM)
    return pl.pallas_call(
        pair_kernel,
        out_shape=jax.ShapeDtypeStruct((16, 32, 1152), bf16),
        in_specs=[pl.BlockSpec(memory_space=pltpu.SMEM)] + [vmem] * 6,
        out_specs=vmem,
        scratch_shapes=[pltpu.VMEM((128, 128), f32)],
        compiler_params=pltpu.CompilerParams(vmem_limit_bytes=16 * 1024 * 1024),
        cost_estimate=pl.CostEstimate(flops=270_000_000, bytes_accessed=2_000_000, transcendentals=0),
        name="pair_terms",
    )(core, keep, other, d_field, d_other, note, note_other)


def plane_kernel(group_ref, terms_ref, *rest):
    outs, tint_ref = rest[:4], rest[4]
    total = terms_ref[0, :, 0:1024].astype(f32)
    gain = jnp.zeros((8, 128), f32)
    for i in range(terms_ref.shape[0]):
        if i:
            total = total + terms_ref[i, :, 0:1024].astype(f32)
        extra = terms_ref[i, :, 1024:1152].astype(f32)
        gain = gain + (extra[8:16, :] + extra[16:24, :])
        tint = extra[0:4, :] + extra[4:8, :]
        for z in range(4):
            tint_ref[z, i : i + 1, :] = tint[z : z + 1, :]
    total = total.astype(bf16)
    gain_rows = jnp.concatenate([*two_terms(gain), jnp.zeros((16, 128), f32)], axis=0).astype(bf16)
    for k, out in enumerate(outs):
        out[:, 0:1024] = total
        tint = tint_ref[jnp.bitwise_and(group_ref[0] + k, 3)]
        out[:, 1024:1152] = jnp.concatenate(two_terms(tint), axis=0).astype(bf16)
        out[:, 1152:1280] = gain_rows


def plane_sum(group, terms):
    vmem = pl.BlockSpec(memory_space=pltpu.VMEM)
    return pl.pallas_call(
        plane_kernel,
        out_shape=(jax.ShapeDtypeStruct((32, 1280), bf16),) * 4,
        in_specs=[pl.BlockSpec(memory_space=pltpu.SMEM), vmem],
        out_specs=(vmem,) * 4,
        scratch_shapes=[pltpu.VMEM((4, 16, 128), f32)],
        cost_estimate=pl.CostEstimate(flops=1_000_000, bytes_accessed=1_500_000, transcendentals=0),
        name="plane_sum",
    )(group, terms)


def finish_kernel(group_ref, slot_ref, m0, m1, m2, m3, color_ref, loss_ref, head_ref, gain_out_ref, tint_ref, rows_ref):
    rays = color_ref.shape[1]
    planes = (m0, m1, m2, m3)

    def summed(parts):
        return (parts[0] + parts[2]) + (parts[1] + parts[3])

    head_ref[...] = summed([m[:, 0:1024].astype(f32) for m in planes])
    gains = [m[:, 1152:1280].astype(f32) for m in planes]
    gain_out_ref[...] = summed([g[0:8, :] + g[8:16, :] for g in gains])
    losses = []
    for k, m in enumerate(planes):
        tint = m[:, 1024:1152].astype(f32)
        tint = tint[0:16, :] + tint[16:32, :]
        losses.append(jnp.sum(tint, axis=0, keepdims=True))
        for i in range(16):
            tint_ref[k * 16 + i] = tint[i : i + 1, :]
    lane = lax.broadcasted_iota(jnp.int32, (1, 128), 1)
    loss = jnp.where(jnp.logical_or(lane == 6, lane == 14), summed(losses), 0.0)
    loss_ref[...] = jnp.sum(loss, axis=1, keepdims=True)
    for r in range(rays):
        slot = slot_ref[r]
        scene = lax.shift_right_logical(slot, 1)
        turn = jnp.bitwise_and(group_ref[0] - lax.shift_right_logical(scene, 5), 3)
        row = turn * 16 + jnp.bitwise_and(lax.shift_right_logical(scene, 1), 15)
        first = 8 * jnp.bitwise_and(scene, 1) + 3 * jnp.bitwise_and(slot, 1)
        kept = jnp.logical_and(lane >= first, lane < first + 3)
        rows_ref[r : r + 1, :] = jnp.where(kept, tint_ref[row], 0.0)
    turned = rows_ref[...].T
    color_ref[...] = (turned[0:3, :] + turned[3:6, :]) + (turned[8:11, :] + turned[11:14, :])


def finish(group, slot, planes):
    vmem = pl.BlockSpec(memory_space=pltpu.VMEM)
    smem = pl.BlockSpec(memory_space=pltpu.SMEM)
    rays = slot.shape[0]
    return pl.pallas_call(
        finish_kernel,
        out_shape=(
            jax.ShapeDtypeStruct((3, rays), f32),
            jax.ShapeDtypeStruct((1, 1), f32),
            jax.ShapeDtypeStruct((32, 1024), f32),
            jax.ShapeDtypeStruct((8, 128), f32),
        ),
        in_specs=[smem, smem] + [vmem] * 4,
        out_specs=(vmem,) * 4,
        scratch_shapes=[pltpu.VMEM((64, 1, 128), f32), pltpu.VMEM((rays, 128), f32)],
        cost_estimate=pl.CostEstimate(flops=300_000, bytes_accessed=500_000, transcendentals=0),
        name="finish",
    )(group, slot, *planes)


def body(
    latents,
    head_weight,
    norm_gain,
    color_head,
    sample_points,
    sample_spacing,
    ray_targets,
    ray_scene,
):
    slots = lax.axis_size(both)
    shards = lax.axis_size("shard")
    groups = lax.axis_size("grp")
    core = jnp.bitwise_and(lax.axis_index("shard"), 1).reshape(1).astype(jnp.int32)
    group = lax.axis_index("grp").reshape(1).astype(jnp.int32)
    gain_line = norm_gain[None, :]
    same_core = [[i for i in range(shards) if i % 2 == c] for c in range(2)]
    across = [(i, i ^ 1) for i in range(shards)]

    def among_same_core(x):
        return lax.all_to_all(x, "shard", split_axis=0, concat_axis=0, tiled=True, axis_index_groups=same_core)

    own_rows = among_same_core(jnp.broadcast_to(head_weight[None], (shards // 2, *head_weight.shape)))
    own_rows = own_rows.reshape(512, 1024)
    sent, slot = pack(ray_scene, sample_points, sample_spacing, ray_targets, slots)
    sent, own_rows = lax.optimization_barrier((sent, own_rows))
    other_rows = lax.ppermute(own_rows, "shard", across)
    recv = lax.all_to_all(sent, both, split_axis=0, concat_axis=0, tiled=True).reshape(slots, 640)
    weight, w0t, w1, w1t, keep, send = make_field(core, latents, own_rows, other_rows, gain_line)
    x_other = lax.ppermute(send, "shard", across)
    colors, d_field = render(recv, w0t, w1, w1t, color_head)
    d_other = lax.ppermute(d_field, "shard", across)
    latent_grad, note = latent_gradient(latents, weight, gain_line, d_field, colors)
    note_other = lax.ppermute(note, "shard", across)
    paired = pair_terms(core, keep, x_other, d_field, d_other, note, note_other)
    planes = plane_sum(group, among_same_core(paired))
    planes = [planes[0]] + [
        lax.ppermute(planes[k], "grp", [(i, (i + k) % groups) for i in range(groups)]) for k in range(1, groups)
    ]
    rendered, loss, head_grad, gain_grad = finish(group, slot, planes)
    return (rendered, loss.reshape(()), head_grad, gain_grad.reshape(-1), latent_grad)


def solution(mesh):
    placed = (
        P(both, None),
        P("shard", None),
        P(),
        P(),
        P(both, None),
        P(both, None),
        P(None, both),
        P(both),
    )
    return jax.shard_map(
        body,
        mesh=mesh,
        in_specs=placed,
        out_specs=(
            P(None, both),
            P(),
            P("shard", None),
            P(),
            P(both, None),
        ),
        check_vma=False,
    )
```

```python
import jax
import jax.numpy as jnp
from jax import lax
from jax.experimental import pallas as pl
from jax.experimental.pallas import tpu as pltpu
from jax.sharding import PartitionSpec as P

norm_eps = 1e-06
f32, bf16 = jnp.float32, jnp.bfloat16
both = ("grp", "shard")

sin_coef = (3.141590256747904, -5.167405766362, 2.544000216186916, -0.5594350008327638)
cos_coef = (0.999999953027512, -4.934792802489427, 4.058410790762133, -1.3318729727851486, 0.21968242357146)

step_block = 8
features = 48


def fold_matrix():
    m = lax.broadcasted_iota(jnp.int32, (features, 256), 0).astype(f32)
    i = lax.broadcasted_iota(jnp.int32, (features, 256), 1).astype(f32)
    q = jnp.floor(i * (1 / 64) + 1 / 128)
    j = 4.0 * (i - 64.0 * q) + q
    jm = j - features * jnp.floor((j + 0.5) * (1 / features))
    coordinate = jnp.floor((m + 0.5) * (1 / 16))
    phase = jnp.floor((m - 16.0 * coordinate + 0.5) * (1 / 8))
    octave = m - 16.0 * coordinate - 8.0 * phase
    return (jm == coordinate + 3.0 * phase + 6.0 * octave).astype(f32)


def dot(a, b, dims=(((1,), (0,)), ((), ())), precision=None):
    return lax.dot_general(a, b, dims, preferred_element_type=f32, precision=precision)


def pack_kernel(place_ref, scene_ref, points_ref, spacing_ref, target_ref, *rest):
    outs, (slot_ref, count_ref, row_ref, pay_ref, tint_ref) = rest[:8], rest[8:]
    rays = points_ref.shape[0]
    group, core = place_ref[0], place_ref[1]
    for d in range(count_ref.shape[0]):
        count_ref[d] = 0
    row_ref[...] = jnp.zeros_like(row_ref)
    pay_ref[:, 0:192] = points_ref[...]
    pay_ref[:, 192:256] = spacing_ref[...]
    target = jnp.concatenate([target_ref[...], jnp.zeros((5, rays), f32)], axis=0).T
    lane = lax.broadcasted_iota(jnp.int32, (rays, 128), 1)
    for k in range(2):
        placed = jnp.zeros((rays, 128), f32)
        for c in range(3):
            placed = jnp.where(lane == 3 * k + c, target[:, c : c + 1], placed)
        tint_ref[k] = placed

    for r in range(rays):
        scene = scene_ref[r]
        rank = count_ref[scene]
        count_ref[scene] = rank + 1
        slot_ref[r] = scene * 2 + rank
        turn = jnp.bitwise_and(lax.shift_right_logical(scene, 5) - group, 3)
        side = jnp.bitwise_and(scene + core, 1)
        row = (turn * 2 + side) * 16 + jnp.bitwise_and(lax.shift_right_logical(scene, 1), 15)
        row_ref[row, :, pl.ds(pl.multiple_of(rank * 256, 256), 256)] = pay_ref[r : r + 1, :]
        row_ref[row, :, 512:640] += tint_ref[rank, r : r + 1, :]
    for n, out in enumerate(outs):
        out[...] = row_ref[n * 16 : (n + 1) * 16]


def pack(place, ray_scene, points, spacing, targets, slots):
    rays = points.shape[0]
    smem = pl.BlockSpec(memory_space=pltpu.SMEM)
    vmem = pl.BlockSpec(memory_space=pltpu.VMEM)
    return pl.pallas_call(
        pack_kernel,
        out_shape=(
            *(jax.ShapeDtypeStruct((slots // 8, 1, 640), f32),) * 8,
            jax.ShapeDtypeStruct((rays,), jnp.int32),
        ),
        in_specs=[smem, smem] + [vmem] * 3,
        out_specs=(*(vmem,) * 8, smem),
        scratch_shapes=[
            pltpu.SMEM((slots,), jnp.int32),
            pltpu.VMEM((slots, 1, 640), f32),
            pltpu.VMEM((rays, 256), f32),
            pltpu.VMEM((2, rays, 128), f32),
        ],
        cost_estimate=pl.CostEstimate(flops=200000, bytes_accessed=1000000, transcendentals=0),
        name="pack",
    )(place, ray_scene, points, spacing, targets)


def stack_kernel(place_ref, *rest):
    parts, out_ref = rest[:8], rest[8]
    group, core = place_ref[0], place_ref[1]
    for n, part in enumerate(parts):
        source = jnp.bitwise_and(group - n // 2, 3) * 2 + jnp.bitwise_and(core + n, 1)
        for i in range(16):
            out_ref[i, source] = part[i]


def stack(place, parts):
    vmem = pl.BlockSpec(memory_space=pltpu.VMEM)
    return pl.pallas_call(
        stack_kernel,
        out_shape=jax.ShapeDtypeStruct((16, 8, 1, 640), f32),
        in_specs=[pl.BlockSpec(memory_space=pltpu.SMEM)] + [vmem] * 8,
        out_specs=vmem,
        cost_estimate=pl.CostEstimate(flops=100_000, bytes_accessed=800_000, transcendentals=0),
        name="stack",
    )(place, *parts)


def copies_kernel(rows_ref, out_ref):
    rows = rows_ref[...]
    for i in range(out_ref.shape[0]):
        out_ref[i] = rows


def copies(rows, count):
    vmem = pl.BlockSpec(memory_space=pltpu.VMEM)
    return pl.pallas_call(
        copies_kernel,
        out_shape=jax.ShapeDtypeStruct((count, *rows.shape), rows.dtype),
        in_specs=[vmem],
        out_specs=vmem,
        cost_estimate=pl.CostEstimate(flops=0, bytes_accessed=1_000_000, transcendentals=0),
        name="copies",
    )(rows)


def field_kernel(
    core_ref,
    latent_ref,
    own_ref,
    other_ref,
    gain_ref,
    weight_ref,
    w0t_ref,
    w1_ref,
    w1t_ref,
    keep_ref,
    send_ref,
    rows_ref,
    turned_ref,
):
    scale = 1.0 / 16.0
    own = core_ref[0]
    for i in range(16):
        for part, ref in ((own, own_ref), (1 - own, other_ref)):
            weight_ref[pl.ds(pl.multiple_of(i * 64 + part * 32, 32), 32), :] = ref[i * 32 : (i + 1) * 32, :]
    latent = latent_ref[...].astype(f32)
    inv_rms = lax.rsqrt(jnp.mean(latent * latent, axis=1, keepdims=True) + norm_eps)
    normed = latent * inv_rms * gain_ref[...]
    field = dot(normed.astype(bf16), weight_ref[...]).astype(bf16)
    stacked = jnp.concatenate([field[0:64, q * 256 : (q + 1) * 256] for q in range(4)], axis=0)
    folded = dot(fold_matrix().astype(bf16), stacked) * scale
    high = folded.astype(bf16).astype(f32)
    split = jnp.concatenate([high, folded - high, jnp.zeros((32, 256), f32)], axis=0)
    w0t_ref[...] = split.T.astype(bf16)
    field1 = field[64:128, :].astype(f32) * scale
    for q in range(4):
        for n in range(2):
            rows_ref[n, pl.ds(q, 64, stride=4), :] = field1[:, q * 256 + n * 128 : q * 256 + (n + 1) * 128]
    w1f = jnp.concatenate([rows_ref[0], rows_ref[1]], axis=1)
    w1_ref[...] = w1f.astype(bf16)
    w1t_ref[...] = w1f.T.astype(bf16)
    turned_ref[...] = normed.T.astype(bf16)
    for out, part in ((keep_ref, own), (send_ref, 1 - own)):
        for i in range(16):
            out[i * 32 : (i + 1) * 32, :] = turned_ref[pl.ds(pl.multiple_of(i * 64 + part * 32, 32), 32), :]


def make_field(core, latents, own_rows, other_rows, gain):
    vmem = pl.BlockSpec(memory_space=pltpu.VMEM)
    shapes = ((1024, 1024), (256, 128), (256, 256), (256, 256), (512, 128), (512, 128))
    return pl.pallas_call(
        field_kernel,
        out_shape=tuple(jax.ShapeDtypeStruct(shape, bf16) for shape in shapes),
        in_specs=[pl.BlockSpec(memory_space=pltpu.SMEM)] + [vmem] * 4,
        out_specs=(vmem,) * 6,
        scratch_shapes=[pltpu.VMEM((2, 256, 128), f32), pltpu.VMEM((1024, 128), bf16)],
        compiler_params=pltpu.CompilerParams(vmem_limit_bytes=24 * 1024 * 1024),
        cost_estimate=pl.CostEstimate(flops=400_000_000, bytes_accessed=5_000_000, transcendentals=0),
        name="field",
    )(core, latents, own_rows, other_rows, gain)


def horner(u, coef):
    value = coef[-1] * u + coef[-2]
    for c in coef[-3::-1]:
        value = value * u + c
    return value


def render_kernel(
    recv_ref,
    w0t_ref,
    w1_ref,
    w1t_ref,
    head_ref,
    color_ref,
    dfield_ref,
    rays_ref,
    h0_ref,
    h1_ref,
    h2_ref,
    raw_ref,
    draw_ref,
    g0_ref,
    g1_ref,
    rows_ref,
):
    scale = 1.0 / 16.0
    slots = recv_ref.shape[0]
    rays = 2 * slots
    blocks = 64 // step_block

    for k in range(2):
        rays_ref[0:256, k * slots : (k + 1) * slots] = recv_ref[:, k * 256 : (k + 1) * 256].T
    tint = recv_ref[:, 512:640].T
    w0t = w0t_ref[:, 0:96]
    w1 = w1_ref[...]
    w1t = w1t_ref[...]
    head_f = jnp.concatenate([head_ref[...].astype(f32), jnp.zeros((4, 256), f32)], axis=0)
    head = head_f.astype(bf16)
    head_t = (head_f * scale).T.astype(bf16)

    octave = jnp.left_shift(1, lax.broadcasted_iota(jnp.int32, (8, rays), 0)).astype(f32)

    def forward(b, carry):
        parts = [[] for _ in range(6)]
        for c in range(3):
            group = rays_ref[pl.ds(pl.multiple_of(c * 64 + b * step_block, 8), step_block), :]
            for s in range(step_block):
                y = group[s : s + 1, :] * octave
                whole = jnp.floor(y + 0.5)
                r = y - whole
                half = whole * 0.5
                sign = 1.0 - 4.0 * (half - jnp.floor(half))
                u = r * r
                parts[2 * c].append(r * sign * horner(u, sin_coef))
                parts[2 * c + 1].append(sign * horner(u, cos_coef))
        h0 = jnp.concatenate([jnp.concatenate(p, axis=1) for p in parts], axis=0).astype(bf16)
        h0_ref[b] = h0
        h1 = jnp.maximum(dot(w0t, jnp.concatenate([h0, h0], axis=0)), 0.0).astype(bf16)
        h1_ref[b] = h1
        h2 = jnp.maximum(dot(w1t, h1), 0.0).astype(bf16)
        h2_ref[b] = h2
        raw = dot(head, h2)
        for s in range(step_block):
            at = pl.ds(pl.multiple_of((b * step_block + s) * 8, 8), 8)
            for k in range(2):
                raw_ref[k, at, :] = raw[:, (2 * s + k) * slots : (2 * s + k + 1) * slots]
        return carry

    lax.fori_loop(0, blocks, forward, 0, unroll=True)

    def spread(c):
        return jnp.concatenate([raw_ref[k, pl.ds(c, 64, stride=8), :] for k in range(2)], axis=1)

    def store_gradient(c, value):
        for k in range(2):
            draw_ref[k, pl.ds(c, 64, stride=8), :] = value[:, k * slots : (k + 1) * slots]

    spacing = rays_ref[192:256, :]
    row = lax.broadcasted_iota(jnp.int32, (64, 64), 0)
    column = lax.broadcasted_iota(jnp.int32, (64, 64), 1)
    raw0 = spread(0)
    density = jnp.maximum(raw0, 0.0) + jnp.log1p(jnp.exp(-jnp.abs(raw0)))
    optical = density * spacing
    before = dot((column < row).astype(f32), optical, precision=lax.Precision.HIGHEST)
    transmit = jnp.exp(-before)
    survive = jnp.exp(-optical)
    blend = transmit * (1.0 - survive)
    live = (spacing[0:1, :] > 0.0).astype(f32)
    factor = 1.0 / (float(slots) * jnp.sum(live, axis=1, keepdims=True))
    albedo = [jax.nn.sigmoid(spread(1 + c)) for c in range(3)]
    d_blend = jnp.zeros_like(blend)
    square = jnp.zeros_like(live)
    colors, grads = [], []
    for c in range(3):
        color = jnp.sum(blend * (albedo[c] - 1.0), axis=0, keepdims=True) + 1.0
        target = jnp.concatenate([tint[c : c + 1, :], tint[3 + c : 4 + c, :]], axis=1)
        residual = (color - target) * live
        square = square + residual * residual
        grad = 2.0 * residual * factor
        d_blend = d_blend + grad * (albedo[c] - 1.0)
        colors.append(color)
        grads.append(grad)
    loss = jnp.sum(square, axis=1, keepdims=True) * factor
    rows = [colors[c][:, k * slots : (k + 1) * slots] for k in range(2) for c in range(3)]
    color_ref[...] = jnp.concatenate([*rows, jnp.broadcast_to(loss, (2, slots))], axis=0)
    weighted = d_blend * blend
    behind = dot((column > row).astype(f32), weighted, precision=lax.Precision.HIGHEST)
    d_optical = d_blend * transmit * survive - behind
    draw_ref[...] = jnp.zeros_like(draw_ref)
    store_gradient(0, d_optical * spacing * jax.nn.sigmoid(raw0))
    for c in range(3):
        store_gradient(1 + c, grads[c] * blend * albedo[c] * (1.0 - albedo[c]))

    g0_ref[...] = jnp.zeros_like(g0_ref)
    g1_ref[...] = jnp.zeros_like(g1_ref)
    on_lanes = (((1,), (1,)), ((), ()))

    def backward(b, carry):
        d_raw = jnp.concatenate(
            [
                draw_ref[k, pl.ds(pl.multiple_of((b * step_block + s) * 8, 8), 8), :]
                for s in range(step_block)
                for k in range(2)
            ],
            axis=1,
        ).astype(bf16)
        h1 = h1_ref[b]
        d_a2 = jnp.where(h2_ref[b] > 0, dot(head_t, d_raw).astype(bf16), jnp.zeros((), bf16))
        d_a1 = jnp.where(h1 > 0, dot(w1, d_a2).astype(bf16), jnp.zeros((), bf16))
        g1_ref[...] += dot(h1, d_a2, on_lanes)
        g0_ref[...] += dot(h0_ref[b], d_a1, on_lanes)
        return carry

    lax.fori_loop(0, blocks, backward, 0, unroll=True)

    unfold = jnp.concatenate([fold_matrix(), jnp.zeros((80, 256), f32)], axis=0).T[:, 0:features].astype(bf16)
    g0 = dot(unfold, g0_ref[...].astype(bf16)).astype(bf16)
    for n in range(2):
        rows_ref[n] = g1_ref[:, n * 128 : (n + 1) * 128]
    for q in range(4):
        dfield_ref[0:64, q * 256 : (q + 1) * 256] = g0[q * 64 : (q + 1) * 64, :]
        for n in range(2):
            at = slice(q * 256 + n * 128, q * 256 + (n + 1) * 128)
            dfield_ref[64:128, at] = rows_ref[n, pl.ds(q, 64, stride=4), :].astype(bf16)


def render(recv, w0t, w1, w1t, head):
    slots = recv.shape[0]
    rays = 2 * slots
    blocks, wide = 64 // step_block, step_block * rays
    vmem = pl.BlockSpec(memory_space=pltpu.VMEM)
    return pl.pallas_call(
        render_kernel,
        out_shape=(
            jax.ShapeDtypeStruct((8, slots), f32),
            jax.ShapeDtypeStruct((128, 1024), bf16),
        ),
        in_specs=[vmem] * 5,
        out_specs=(vmem,) * 2,
        scratch_shapes=[
            pltpu.VMEM((256, rays), f32),
            pltpu.VMEM((blocks, features, wide), bf16),
            pltpu.VMEM((blocks, 256, wide), bf16),
            pltpu.VMEM((blocks, 256, wide), bf16),
            pltpu.VMEM((2, 512, slots), f32),
            pltpu.VMEM((2, 512, slots), f32),
            pltpu.VMEM((features, 256), f32),
            pltpu.VMEM((256, 256), f32),
            pltpu.VMEM((2, 256, 128), f32),
        ],
        compiler_params=pltpu.CompilerParams(vmem_limit_bytes=44 * 1024 * 1024),
        cost_estimate=pl.CostEstimate(flops=12_000_000_000, bytes_accessed=2_000_000, transcendentals=1_000_000),
        name="render",
    )(recv, w0t, w1, w1t, head)


def latent_kernel(latent_ref, weight_ref, gain_ref, dfield_ref, color_ref, out_ref, note_ref):
    latent = latent_ref[...].astype(f32)
    inv_rms = lax.rsqrt(jnp.mean(latent * latent, axis=1, keepdims=True) + norm_eps)
    x_hat = latent * inv_rms
    d_norm = dot(dfield_ref[...], weight_ref[...], (((1,), (1,)), ((), ())))
    term = d_norm * x_hat
    gain = jnp.sum(term, axis=0, keepdims=True)
    mean = jnp.mean(term * gain_ref[...], axis=1, keepdims=True)
    out_ref[...] = (inv_rms * (d_norm * gain_ref[...] - x_hat * mean)).astype(bf16)
    note_ref[0:8, :] = color_ref[...]
    for i in range(8):
        note_ref[8 + i : 9 + i, :] = gain[:, i * 128 : (i + 1) * 128]


def latent_gradient(latents, weight, gain, d_field, colors):
    vmem = pl.BlockSpec(memory_space=pltpu.VMEM)
    return pl.pallas_call(
        latent_kernel,
        out_shape=(
            jax.ShapeDtypeStruct(latents.shape, bf16),
            jax.ShapeDtypeStruct((16, 128), f32),
        ),
        in_specs=[vmem] * 5,
        out_specs=(vmem,) * 2,
        compiler_params=pltpu.CompilerParams(vmem_limit_bytes=24 * 1024 * 1024),
        cost_estimate=pl.CostEstimate(flops=300_000_000, bytes_accessed=3_000_000, transcendentals=0),
        name="latent_gradient",
    )(latents, weight, gain, d_field, colors)


def two_terms(value):
    high = value.astype(bf16).astype(f32)
    return high, value - high


def pair_kernel(
    core_ref, keep_ref, other_ref, dfield_ref, dother_ref, note_ref, nother_ref, out_ref, turned_ref
):
    first = core_ref[0] == 0
    mine, mate = note_ref[...], nother_ref[...]
    colors = jnp.concatenate(
        [jnp.where(first, mine, mate)[0:8, :], jnp.where(first, mate, mine)[0:8, :], jnp.zeros((112, 128), f32)],
        axis=0,
    )
    turned_ref[...] = colors.T
    gain = two_terms(mine[8:16, :] + mate[8:16, :])
    terms = (dot(keep_ref[...], dfield_ref[...]) + dot(other_ref[...], dother_ref[...])).astype(bf16)
    for i in range(16):
        out_ref[i, :, 0:1024] = terms[i * 32 : (i + 1) * 32, :]
        rows = [turned_ref[pl.ds(8 * i + c, 4, stride=2), :] for c in range(2)]
        tint = two_terms(jnp.where(first, *rows))
        out_ref[i, :, 1024:1152] = jnp.concatenate(
            [*tint, *gain, jnp.zeros((8, 128), f32)], axis=0
        ).astype(bf16)


def pair_terms(core, keep, other, d_field, d_other, note, note_other):
    vmem = pl.BlockSpec(memory_space=pltpu.VMEM)
    return pl.pallas_call(
        pair_kernel,
        out_shape=jax.ShapeDtypeStruct((16, 32, 1152), bf16),
        in_specs=[pl.BlockSpec(memory_space=pltpu.SMEM)] + [vmem] * 6,
        out_specs=vmem,
        scratch_shapes=[pltpu.VMEM((128, 128), f32)],
        compiler_params=pltpu.CompilerParams(vmem_limit_bytes=16 * 1024 * 1024),
        cost_estimate=pl.CostEstimate(flops=270_000_000, bytes_accessed=2_000_000, transcendentals=0),
        name="pair_terms",
    )(core, keep, other, d_field, d_other, note, note_other)


def plane_kernel(group_ref, terms_ref, *rest):
    outs, tint_ref = rest[:4], rest[4]
    total = terms_ref[0, :, 0:1024].astype(f32)
    gain = jnp.zeros((8, 128), f32)
    for i in range(terms_ref.shape[0]):
        if i:
            total = total + terms_ref[i, :, 0:1024].astype(f32)
        extra = terms_ref[i, :, 1024:1152].astype(f32)
        gain = gain + (extra[8:16, :] + extra[16:24, :])
        tint = extra[0:4, :] + extra[4:8, :]
        for z in range(4):
            tint_ref[z, i : i + 1, :] = tint[z : z + 1, :]
    total = total.astype(bf16)
    gain_rows = jnp.concatenate([*two_terms(gain), jnp.zeros((16, 128), f32)], axis=0).astype(bf16)
    for k, out in enumerate(outs):
        out[:, 0:1024] = total
        tint = tint_ref[jnp.bitwise_and(group_ref[0] + k, 3)]
        out[:, 1024:1152] = jnp.concatenate(two_terms(tint), axis=0).astype(bf16)
        out[:, 1152:1280] = gain_rows


def plane_sum(group, terms):
    vmem = pl.BlockSpec(memory_space=pltpu.VMEM)
    return pl.pallas_call(
        plane_kernel,
        out_shape=(jax.ShapeDtypeStruct((32, 1280), bf16),) * 4,
        in_specs=[pl.BlockSpec(memory_space=pltpu.SMEM), vmem],
        out_specs=(vmem,) * 4,
        scratch_shapes=[pltpu.VMEM((4, 16, 128), f32)],
        cost_estimate=pl.CostEstimate(flops=1_000_000, bytes_accessed=1_500_000, transcendentals=0),
        name="plane_sum",
    )(group, terms)


def finish_kernel(group_ref, slot_ref, m0, m1, m2, m3, color_ref, loss_ref, head_ref, gain_out_ref, tint_ref, rows_ref):
    rays = color_ref.shape[1]
    planes = (m0, m1, m2, m3)

    def summed(parts):
        return (parts[0] + parts[2]) + (parts[1] + parts[3])

    head_ref[...] = summed([m[:, 0:1024].astype(f32) for m in planes])
    gains = [m[:, 1152:1280].astype(f32) for m in planes]
    gain_out_ref[...] = summed([g[0:8, :] + g[8:16, :] for g in gains])
    losses = []
    for k, m in enumerate(planes):
        tint = m[:, 1024:1152].astype(f32)
        tint = tint[0:16, :] + tint[16:32, :]
        losses.append(jnp.sum(tint, axis=0, keepdims=True))
        for i in range(16):
            tint_ref[k * 16 + i] = tint[i : i + 1, :]
    lane = lax.broadcasted_iota(jnp.int32, (1, 128), 1)
    loss = jnp.where(jnp.logical_or(lane == 6, lane == 14), summed(losses), 0.0)
    loss_ref[...] = jnp.sum(loss, axis=1, keepdims=True)
    for r in range(rays):
        slot = slot_ref[r]
        scene = lax.shift_right_logical(slot, 1)
        turn = jnp.bitwise_and(group_ref[0] - lax.shift_right_logical(scene, 5), 3)
        row = turn * 16 + jnp.bitwise_and(lax.shift_right_logical(scene, 1), 15)
        first = 8 * jnp.bitwise_and(scene, 1) + 3 * jnp.bitwise_and(slot, 1)
        kept = jnp.logical_and(lane >= first, lane < first + 3)
        rows_ref[r : r + 1, :] = jnp.where(kept, tint_ref[row], 0.0)
    turned = rows_ref[...].T
    color_ref[...] = (turned[0:3, :] + turned[3:6, :]) + (turned[8:11, :] + turned[11:14, :])


def finish(group, slot, planes):
    vmem = pl.BlockSpec(memory_space=pltpu.VMEM)
    smem = pl.BlockSpec(memory_space=pltpu.SMEM)
    rays = slot.shape[0]
    return pl.pallas_call(
        finish_kernel,
        out_shape=(
            jax.ShapeDtypeStruct((3, rays), f32),
            jax.ShapeDtypeStruct((1, 1), f32),
            jax.ShapeDtypeStruct((32, 1024), f32),
            jax.ShapeDtypeStruct((8, 128), f32),
        ),
        in_specs=[smem, smem] + [vmem] * 4,
        out_specs=(vmem,) * 4,
        scratch_shapes=[pltpu.VMEM((64, 1, 128), f32), pltpu.VMEM((rays, 128), f32)],
        cost_estimate=pl.CostEstimate(flops=300_000, bytes_accessed=500_000, transcendentals=0),
        name="finish",
    )(group, slot, *planes)


def body(
    latents,
    head_weight,
    norm_gain,
    color_head,
    sample_points,
    sample_spacing,
    ray_targets,
    ray_scene,
):
    slots = lax.axis_size(both)
    shards = lax.axis_size("shard")
    groups = lax.axis_size("grp")
    core = jnp.bitwise_and(lax.axis_index("shard"), 1).reshape(1).astype(jnp.int32)
    group = lax.axis_index("grp").reshape(1).astype(jnp.int32)
    gain_line = norm_gain[None, :]
    same_core = [[i for i in range(shards) if i % 2 == c] for c in range(2)]
    across = [(i, i ^ 1) for i in range(shards)]

    def among_same_core(x):
        return lax.all_to_all(x, "shard", split_axis=0, concat_axis=0, tiled=True, axis_index_groups=same_core)

    place = jnp.concatenate([group, core])
    *parts, slot = pack(place, ray_scene, sample_points, sample_spacing, ray_targets, slots)
    own_rows = among_same_core(copies(head_weight, shards // 2))
    own_rows = own_rows.reshape(512, 1024)
    for n in range(1, 8):
        moves = [
            (z * shards + i, (z + n // 2) % groups * shards + (i ^ (n % 2))) for z in range(groups) for i in range(shards)
        ]
        parts[n] = lax.ppermute(parts[n], both, moves)
    sent, own_rows = lax.optimization_barrier((stack(place, parts), own_rows))
    other_rows = lax.ppermute(own_rows, "shard", across)
    recv = among_same_core(sent).reshape(slots, 640)
    weight, w0t, w1, w1t, keep, send = make_field(core, latents, own_rows, other_rows, gain_line)
    x_other = lax.ppermute(send, "shard", across)
    colors, d_field = render(recv, w0t, w1, w1t, color_head)
    d_other = lax.ppermute(d_field, "shard", across)
    latent_grad, note = latent_gradient(latents, weight, gain_line, d_field, colors)
    note_other = lax.ppermute(note, "shard", across)
    paired = pair_terms(core, keep, x_other, d_field, d_other, note, note_other)
    planes = plane_sum(group, among_same_core(paired))
    planes = [planes[0]] + [
        lax.ppermute(planes[k], "grp", [(i, (i + k) % groups) for i in range(groups)]) for k in range(1, groups)
    ]
    rendered, loss, head_grad, gain_grad = finish(group, slot, planes)
    return (rendered, loss.reshape(()), head_grad, gain_grad.reshape(-1), latent_grad)


def solution(mesh):
    placed = (
        P(both, None),
        P("shard", None),
        P(),
        P(),
        P(both, None),
        P(both, None),
        P(None, both),
        P(both),
    )
    return jax.shard_map(
        body,
        mesh=mesh,
        in_specs=placed,
        out_specs=(
            P(None, both),
            P(),
            P("shard", None),
            P(),
            P(both, None),
        ),
        check_vma=False,
    )
```

```python
import jax
import jax.numpy as jnp
from jax import lax
from jax.experimental import pallas as pl
from jax.experimental.pallas import tpu as pltpu
from jax.sharding import PartitionSpec as P

norm_eps = 1e-06
f32, bf16 = jnp.float32, jnp.bfloat16
both = ("grp", "shard")

sin_coef = (3.141590256747904, -5.167405766362, 2.544000216186916, -0.5594350008327638)
cos_coef = (0.999999953027512, -4.934792802489427, 4.058410790762133, -1.3318729727851486, 0.21968242357146)

step_block = 8
features = 48


def fold_matrix():
    m = lax.broadcasted_iota(jnp.int32, (features, 256), 0).astype(f32)
    i = lax.broadcasted_iota(jnp.int32, (features, 256), 1).astype(f32)
    q = jnp.floor(i * (1 / 64) + 1 / 128)
    j = 4.0 * (i - 64.0 * q) + q
    jm = j - features * jnp.floor((j + 0.5) * (1 / features))
    coordinate = jnp.floor((m + 0.5) * (1 / 16))
    phase = jnp.floor((m - 16.0 * coordinate + 0.5) * (1 / 8))
    octave = m - 16.0 * coordinate - 8.0 * phase
    return (jm == coordinate + 3.0 * phase + 6.0 * octave).astype(f32)


def dot(a, b, dims=(((1,), (0,)), ((), ())), precision=None):
    return lax.dot_general(a, b, dims, preferred_element_type=f32, precision=precision)


def pack_kernel(place_ref, scene_ref, points_ref, spacing_ref, target_ref, *rest):
    outs, (slot_ref, count_ref, row_ref, pay_ref, tint_ref) = rest[:8], rest[8:]
    rays = points_ref.shape[0]
    group, core = place_ref[0], place_ref[1]
    for d in range(count_ref.shape[0]):
        count_ref[d] = 0
    row_ref[...] = jnp.zeros_like(row_ref)
    pay_ref[:, 0:192] = points_ref[...]
    pay_ref[:, 192:256] = spacing_ref[...]
    target = jnp.concatenate([target_ref[...], jnp.zeros((5, rays), f32)], axis=0).T
    lane = lax.broadcasted_iota(jnp.int32, (rays, 128), 1)
    for k in range(2):
        placed = jnp.zeros((rays, 128), f32)
        for c in range(3):
            placed = jnp.where(lane == 3 * k + c, target[:, c : c + 1], placed)
        tint_ref[k] = placed

    for r in range(rays):
        scene = scene_ref[r]
        rank = count_ref[scene]
        count_ref[scene] = rank + 1
        slot_ref[r] = scene * 2 + rank
        turn = jnp.bitwise_and(lax.shift_right_logical(scene, 5) - group, 3)
        side = jnp.bitwise_and(scene + core, 1)
        row = (turn * 2 + side) * 16 + jnp.bitwise_and(lax.shift_right_logical(scene, 1), 15)
        row_ref[row, :, pl.ds(pl.multiple_of(rank * 256, 256), 256)] = pay_ref[r : r + 1, :]
        row_ref[row, :, 512:640] += tint_ref[rank, r : r + 1, :]
    for n, out in enumerate(outs):
        out[...] = row_ref[n * 16 : (n + 1) * 16]


def pack(place, ray_scene, points, spacing, targets, slots):
    rays = points.shape[0]
    smem = pl.BlockSpec(memory_space=pltpu.SMEM)
    vmem = pl.BlockSpec(memory_space=pltpu.VMEM)
    return pl.pallas_call(
        pack_kernel,
        out_shape=(
            *(jax.ShapeDtypeStruct((slots // 8, 1, 640), f32),) * 8,
            jax.ShapeDtypeStruct((rays,), jnp.int32),
        ),
        in_specs=[smem, smem] + [vmem] * 3,
        out_specs=(*(vmem,) * 8, smem),
        scratch_shapes=[
            pltpu.SMEM((slots,), jnp.int32),
            pltpu.VMEM((slots, 1, 640), f32),
            pltpu.VMEM((rays, 256), f32),
            pltpu.VMEM((2, rays, 128), f32),
        ],
        compiler_params=pltpu.CompilerParams(vmem_limit_bytes=4 * 1024 * 1024),
        cost_estimate=pl.CostEstimate(flops=200000, bytes_accessed=1000000, transcendentals=0),
        name="pack",
    )(place, ray_scene, points, spacing, targets)


def stack_kernel(place_ref, *rest):
    parts, out_ref = rest[:8], rest[8]
    group, core = place_ref[0], place_ref[1]
    for n, part in enumerate(parts):
        source = jnp.bitwise_and(group - n // 2, 3) * 2 + jnp.bitwise_and(core + n, 1)
        for i in range(16):
            out_ref[i, source] = part[i]


def stack(place, parts):
    vmem = pl.BlockSpec(memory_space=pltpu.VMEM)
    return pl.pallas_call(
        stack_kernel,
        out_shape=jax.ShapeDtypeStruct((16, 8, 1, 640), f32),
        in_specs=[pl.BlockSpec(memory_space=pltpu.SMEM)] + [vmem] * 8,
        out_specs=vmem,
        compiler_params=pltpu.CompilerParams(vmem_limit_bytes=4 * 1024 * 1024),
        cost_estimate=pl.CostEstimate(flops=100_000, bytes_accessed=800_000, transcendentals=0),
        name="stack",
    )(place, *parts)


def copies_kernel(rows_ref, out_ref):
    rows = rows_ref[...]
    for i in range(out_ref.shape[0]):
        out_ref[i] = rows


def copies(rows, count):
    vmem = pl.BlockSpec(memory_space=pltpu.VMEM)
    return pl.pallas_call(
        copies_kernel,
        out_shape=jax.ShapeDtypeStruct((count, *rows.shape), rows.dtype),
        in_specs=[vmem],
        out_specs=vmem,
        compiler_params=pltpu.CompilerParams(vmem_limit_bytes=4 * 1024 * 1024),
        cost_estimate=pl.CostEstimate(flops=0, bytes_accessed=1_000_000, transcendentals=0),
        name="copies",
    )(rows)


def field_kernel(
    core_ref,
    latent_ref,
    own_ref,
    other_ref,
    gain_ref,
    weight_ref,
    w0t_ref,
    w1_ref,
    w1t_ref,
    keep_ref,
    send_ref,
    rows_ref,
    turned_ref,
):
    scale = 1.0 / 16.0
    own = core_ref[0]
    for i in range(16):
        for part, ref in ((own, own_ref), (1 - own, other_ref)):
            weight_ref[pl.ds(pl.multiple_of(i * 64 + part * 32, 32), 32), :] = ref[i * 32 : (i + 1) * 32, :]
    latent = latent_ref[...].astype(f32)
    inv_rms = lax.rsqrt(jnp.mean(latent * latent, axis=1, keepdims=True) + norm_eps)
    normed = latent * inv_rms * gain_ref[...]
    field = dot(normed.astype(bf16), weight_ref[...]).astype(bf16)
    stacked = jnp.concatenate([field[0:64, q * 256 : (q + 1) * 256] for q in range(4)], axis=0)
    folded = dot(fold_matrix().astype(bf16), stacked) * scale
    high = folded.astype(bf16).astype(f32)
    split = jnp.concatenate([high, folded - high, jnp.zeros((32, 256), f32)], axis=0)
    w0t_ref[...] = split.T.astype(bf16)
    field1 = field[64:128, :].astype(f32) * scale
    for q in range(4):
        for n in range(2):
            rows_ref[n, pl.ds(q, 64, stride=4), :] = field1[:, q * 256 + n * 128 : q * 256 + (n + 1) * 128]
    w1f = jnp.concatenate([rows_ref[0], rows_ref[1]], axis=1)
    w1_ref[...] = w1f.astype(bf16)
    w1t_ref[...] = w1f.T.astype(bf16)
    turned_ref[...] = normed.T.astype(bf16)
    for out, part in ((keep_ref, own), (send_ref, 1 - own)):
        for i in range(16):
            out[i * 32 : (i + 1) * 32, :] = turned_ref[pl.ds(pl.multiple_of(i * 64 + part * 32, 32), 32), :]


def make_field(core, latents, own_rows, other_rows, gain):
    vmem = pl.BlockSpec(memory_space=pltpu.VMEM)
    shapes = ((1024, 1024), (256, 128), (256, 256), (256, 256), (512, 128), (512, 128))
    return pl.pallas_call(
        field_kernel,
        out_shape=tuple(jax.ShapeDtypeStruct(shape, bf16) for shape in shapes),
        in_specs=[pl.BlockSpec(memory_space=pltpu.SMEM)] + [vmem] * 4,
        out_specs=(vmem,) * 6,
        scratch_shapes=[pltpu.VMEM((2, 256, 128), f32), pltpu.VMEM((1024, 128), bf16)],
        compiler_params=pltpu.CompilerParams(vmem_limit_bytes=24 * 1024 * 1024),
        cost_estimate=pl.CostEstimate(flops=400_000_000, bytes_accessed=5_000_000, transcendentals=0),
        name="field",
    )(core, latents, own_rows, other_rows, gain)


def horner(u, coef):
    value = coef[-1] * u + coef[-2]
    for c in coef[-3::-1]:
        value = value * u + c
    return value


def render_kernel(
    recv_ref,
    w0t_ref,
    w1_ref,
    w1t_ref,
    head_ref,
    color_ref,
    dfield_ref,
    rays_ref,
    h0_ref,
    h1_ref,
    h2_ref,
    raw_ref,
    draw_ref,
    g0_ref,
    g1_ref,
    rows_ref,
):
    scale = 1.0 / 16.0
    slots = recv_ref.shape[0]
    rays = 2 * slots
    blocks = 64 // step_block

    for k in range(2):
        rays_ref[0:256, k * slots : (k + 1) * slots] = recv_ref[:, k * 256 : (k + 1) * 256].T
    tint = recv_ref[:, 512:640].T
    w0t = w0t_ref[:, 0:96]
    w1 = w1_ref[...]
    w1t = w1t_ref[...]
    head_f = jnp.concatenate([head_ref[...].astype(f32), jnp.zeros((4, 256), f32)], axis=0)
    head = head_f.astype(bf16)
    head_t = (head_f * scale).T.astype(bf16)

    octave = jnp.left_shift(1, lax.broadcasted_iota(jnp.int32, (8, rays), 0)).astype(f32)

    def forward(b, carry):
        parts = [[] for _ in range(6)]
        for c in range(3):
            group = rays_ref[pl.ds(pl.multiple_of(c * 64 + b * step_block, 8), step_block), :]
            for s in range(step_block):
                y = group[s : s + 1, :] * octave
                whole = jnp.floor(y + 0.5)
                r = y - whole
                half = whole * 0.5
                sign = 1.0 - 4.0 * (half - jnp.floor(half))
                u = r * r
                parts[2 * c].append(r * sign * horner(u, sin_coef))
                parts[2 * c + 1].append(sign * horner(u, cos_coef))
        h0 = jnp.concatenate([jnp.concatenate(p, axis=1) for p in parts], axis=0).astype(bf16)
        h0_ref[b] = h0
        h1 = jnp.maximum(dot(w0t, jnp.concatenate([h0, h0], axis=0)), 0.0).astype(bf16)
        h1_ref[b] = h1
        h2 = jnp.maximum(dot(w1t, h1), 0.0).astype(bf16)
        h2_ref[b] = h2
        raw = dot(head, h2)
        for s in range(step_block):
            at = pl.ds(pl.multiple_of((b * step_block + s) * 8, 8), 8)
            for k in range(2):
                raw_ref[k, at, :] = raw[:, (2 * s + k) * slots : (2 * s + k + 1) * slots]
        return carry

    lax.fori_loop(0, blocks, forward, 0, unroll=True)

    def spread(c):
        return jnp.concatenate([raw_ref[k, pl.ds(c, 64, stride=8), :] for k in range(2)], axis=1)

    def store_gradient(c, value):
        for k in range(2):
            draw_ref[k, pl.ds(c, 64, stride=8), :] = value[:, k * slots : (k + 1) * slots]

    spacing = rays_ref[192:256, :]
    row = lax.broadcasted_iota(jnp.int32, (64, 64), 0)
    column = lax.broadcasted_iota(jnp.int32, (64, 64), 1)
    raw0 = spread(0)
    density = jnp.maximum(raw0, 0.0) + jnp.log1p(jnp.exp(-jnp.abs(raw0)))
    optical = density * spacing
    before = dot((column < row).astype(f32), optical, precision=lax.Precision.HIGHEST)
    transmit = jnp.exp(-before)
    survive = jnp.exp(-optical)
    blend = transmit * (1.0 - survive)
    live = (spacing[0:1, :] > 0.0).astype(f32)
    factor = 1.0 / (float(slots) * jnp.sum(live, axis=1, keepdims=True))
    albedo = [jax.nn.sigmoid(spread(1 + c)) for c in range(3)]
    d_blend = jnp.zeros_like(blend)
    square = jnp.zeros_like(live)
    colors, grads = [], []
    for c in range(3):
        color = jnp.sum(blend * (albedo[c] - 1.0), axis=0, keepdims=True) + 1.0
        target = jnp.concatenate([tint[c : c + 1, :], tint[3 + c : 4 + c, :]], axis=1)
        residual = (color - target) * live
        square = square + residual * residual
        grad = 2.0 * residual * factor
        d_blend = d_blend + grad * (albedo[c] - 1.0)
        colors.append(color)
        grads.append(grad)
    loss = jnp.sum(square, axis=1, keepdims=True) * factor
    rows = [colors[c][:, k * slots : (k + 1) * slots] for k in range(2) for c in range(3)]
    color_ref[...] = jnp.concatenate([*rows, jnp.broadcast_to(loss, (2, slots))], axis=0)
    weighted = d_blend * blend
    behind = dot((column > row).astype(f32), weighted, precision=lax.Precision.HIGHEST)
    d_optical = d_blend * transmit * survive - behind
    draw_ref[...] = jnp.zeros_like(draw_ref)
    store_gradient(0, d_optical * spacing * jax.nn.sigmoid(raw0))
    for c in range(3):
        store_gradient(1 + c, grads[c] * blend * albedo[c] * (1.0 - albedo[c]))

    g0_ref[...] = jnp.zeros_like(g0_ref)
    g1_ref[...] = jnp.zeros_like(g1_ref)
    on_lanes = (((1,), (1,)), ((), ()))

    def backward(b, carry):
        d_raw = jnp.concatenate(
            [
                draw_ref[k, pl.ds(pl.multiple_of((b * step_block + s) * 8, 8), 8), :]
                for s in range(step_block)
                for k in range(2)
            ],
            axis=1,
        ).astype(bf16)
        h1 = h1_ref[b]
        d_a2 = jnp.where(h2_ref[b] > 0, dot(head_t, d_raw).astype(bf16), jnp.zeros((), bf16))
        d_a1 = jnp.where(h1 > 0, dot(w1, d_a2).astype(bf16), jnp.zeros((), bf16))
        g1_ref[...] += dot(h1, d_a2, on_lanes)
        g0_ref[...] += dot(h0_ref[b], d_a1, on_lanes)
        return carry

    lax.fori_loop(0, blocks, backward, 0, unroll=True)

    unfold = jnp.concatenate([fold_matrix(), jnp.zeros((80, 256), f32)], axis=0).T[:, 0:features].astype(bf16)
    g0 = dot(unfold, g0_ref[...].astype(bf16)).astype(bf16)
    for n in range(2):
        rows_ref[n] = g1_ref[:, n * 128 : (n + 1) * 128]
    for q in range(4):
        dfield_ref[0:64, q * 256 : (q + 1) * 256] = g0[q * 64 : (q + 1) * 64, :]
        for n in range(2):
            at = slice(q * 256 + n * 128, q * 256 + (n + 1) * 128)
            dfield_ref[64:128, at] = rows_ref[n, pl.ds(q, 64, stride=4), :].astype(bf16)


def render(recv, w0t, w1, w1t, head):
    slots = recv.shape[0]
    rays = 2 * slots
    blocks, wide = 64 // step_block, step_block * rays
    vmem = pl.BlockSpec(memory_space=pltpu.VMEM)
    return pl.pallas_call(
        render_kernel,
        out_shape=(
            jax.ShapeDtypeStruct((8, slots), f32),
            jax.ShapeDtypeStruct((128, 1024), bf16),
        ),
        in_specs=[vmem] * 5,
        out_specs=(vmem,) * 2,
        scratch_shapes=[
            pltpu.VMEM((256, rays), f32),
            pltpu.VMEM((blocks, features, wide), bf16),
            pltpu.VMEM((blocks, 256, wide), bf16),
            pltpu.VMEM((blocks, 256, wide), bf16),
            pltpu.VMEM((2, 512, slots), f32),
            pltpu.VMEM((2, 512, slots), f32),
            pltpu.VMEM((features, 256), f32),
            pltpu.VMEM((256, 256), f32),
            pltpu.VMEM((2, 256, 128), f32),
        ],
        compiler_params=pltpu.CompilerParams(vmem_limit_bytes=44 * 1024 * 1024),
        cost_estimate=pl.CostEstimate(flops=12_000_000_000, bytes_accessed=2_000_000, transcendentals=1_000_000),
        name="render",
    )(recv, w0t, w1, w1t, head)


def latent_kernel(latent_ref, weight_ref, gain_ref, dfield_ref, color_ref, out_ref, note_ref):
    latent = latent_ref[...].astype(f32)
    inv_rms = lax.rsqrt(jnp.mean(latent * latent, axis=1, keepdims=True) + norm_eps)
    x_hat = latent * inv_rms
    d_norm = dot(dfield_ref[...], weight_ref[...], (((1,), (1,)), ((), ())))
    term = d_norm * x_hat
    gain = jnp.sum(term, axis=0, keepdims=True)
    mean = jnp.mean(term * gain_ref[...], axis=1, keepdims=True)
    out_ref[...] = (inv_rms * (d_norm * gain_ref[...] - x_hat * mean)).astype(bf16)
    note_ref[0:8, :] = color_ref[...]
    for i in range(8):
        note_ref[8 + i : 9 + i, :] = gain[:, i * 128 : (i + 1) * 128]


def latent_gradient(latents, weight, gain, d_field, colors):
    vmem = pl.BlockSpec(memory_space=pltpu.VMEM)
    return pl.pallas_call(
        latent_kernel,
        out_shape=(
            jax.ShapeDtypeStruct(latents.shape, bf16),
            jax.ShapeDtypeStruct((16, 128), f32),
        ),
        in_specs=[vmem] * 5,
        out_specs=(vmem,) * 2,
        compiler_params=pltpu.CompilerParams(vmem_limit_bytes=24 * 1024 * 1024),
        cost_estimate=pl.CostEstimate(flops=300_000_000, bytes_accessed=3_000_000, transcendentals=0),
        name="latent_gradient",
    )(latents, weight, gain, d_field, colors)


def two_terms(value):
    high = value.astype(bf16).astype(f32)
    return high, value - high


def pair_kernel(
    core_ref, keep_ref, other_ref, dfield_ref, dother_ref, note_ref, nother_ref, out_ref, turned_ref
):
    first = core_ref[0] == 0
    mine, mate = note_ref[...], nother_ref[...]
    colors = jnp.concatenate(
        [jnp.where(first, mine, mate)[0:8, :], jnp.where(first, mate, mine)[0:8, :], jnp.zeros((112, 128), f32)],
        axis=0,
    )
    turned_ref[...] = colors.T
    gain = two_terms(mine[8:16, :] + mate[8:16, :])
    terms = (dot(keep_ref[...], dfield_ref[...]) + dot(other_ref[...], dother_ref[...])).astype(bf16)
    for i in range(16):
        out_ref[i, :, 0:1024] = terms[i * 32 : (i + 1) * 32, :]
        rows = [turned_ref[pl.ds(8 * i + c, 4, stride=2), :] for c in range(2)]
        tint = two_terms(jnp.where(first, *rows))
        out_ref[i, :, 1024:1152] = jnp.concatenate(
            [*tint, *gain, jnp.zeros((8, 128), f32)], axis=0
        ).astype(bf16)


def pair_terms(core, keep, other, d_field, d_other, note, note_other):
    vmem = pl.BlockSpec(memory_space=pltpu.VMEM)
    return pl.pallas_call(
        pair_kernel,
        out_shape=jax.ShapeDtypeStruct((16, 32, 1152), bf16),
        in_specs=[pl.BlockSpec(memory_space=pltpu.SMEM)] + [vmem] * 6,
        out_specs=vmem,
        scratch_shapes=[pltpu.VMEM((128, 128), f32)],
        compiler_params=pltpu.CompilerParams(vmem_limit_bytes=16 * 1024 * 1024),
        cost_estimate=pl.CostEstimate(flops=270_000_000, bytes_accessed=2_000_000, transcendentals=0),
        name="pair_terms",
    )(core, keep, other, d_field, d_other, note, note_other)


def plane_kernel(group_ref, terms_ref, *rest):
    outs, tint_ref = rest[:4], rest[4]
    total = terms_ref[0, :, 0:1024].astype(f32)
    gain = jnp.zeros((8, 128), f32)
    for i in range(terms_ref.shape[0]):
        if i:
            total = total + terms_ref[i, :, 0:1024].astype(f32)
        extra = terms_ref[i, :, 1024:1152].astype(f32)
        gain = gain + (extra[8:16, :] + extra[16:24, :])
        tint = extra[0:4, :] + extra[4:8, :]
        for z in range(4):
            tint_ref[z, i : i + 1, :] = tint[z : z + 1, :]
    total = total.astype(bf16)
    gain_rows = jnp.concatenate([*two_terms(gain), jnp.zeros((16, 128), f32)], axis=0).astype(bf16)
    for k, out in enumerate(outs):
        out[:, 0:1024] = total
        tint = tint_ref[jnp.bitwise_and(group_ref[0] + k, 3)]
        out[:, 1024:1152] = jnp.concatenate(two_terms(tint), axis=0).astype(bf16)
        out[:, 1152:1280] = gain_rows


def plane_sum(group, terms):
    vmem = pl.BlockSpec(memory_space=pltpu.VMEM)
    return pl.pallas_call(
        plane_kernel,
        out_shape=(jax.ShapeDtypeStruct((32, 1280), bf16),) * 4,
        in_specs=[pl.BlockSpec(memory_space=pltpu.SMEM), vmem],
        out_specs=(vmem,) * 4,
        scratch_shapes=[pltpu.VMEM((4, 16, 128), f32)],
        compiler_params=pltpu.CompilerParams(vmem_limit_bytes=8 * 1024 * 1024),
        cost_estimate=pl.CostEstimate(flops=1_000_000, bytes_accessed=1_500_000, transcendentals=0),
        name="plane_sum",
    )(group, terms)


def finish_kernel(group_ref, slot_ref, m0, m1, m2, m3, color_ref, loss_ref, head_ref, gain_out_ref, tint_ref, rows_ref):
    rays = color_ref.shape[1]
    planes = (m0, m1, m2, m3)

    def summed(parts):
        return (parts[0] + parts[2]) + (parts[1] + parts[3])

    head_ref[...] = summed([m[:, 0:1024].astype(f32) for m in planes])
    gains = [m[:, 1152:1280].astype(f32) for m in planes]
    gain_out_ref[...] = summed([g[0:8, :] + g[8:16, :] for g in gains])
    losses = []
    for k, m in enumerate(planes):
        tint = m[:, 1024:1152].astype(f32)
        tint = tint[0:16, :] + tint[16:32, :]
        losses.append(jnp.sum(tint, axis=0, keepdims=True))
        for i in range(16):
            tint_ref[k * 16 + i] = tint[i : i + 1, :]
    lane = lax.broadcasted_iota(jnp.int32, (1, 128), 1)
    loss = jnp.where(jnp.logical_or(lane == 6, lane == 14), summed(losses), 0.0)
    loss_ref[...] = jnp.sum(loss, axis=1, keepdims=True)
    for r in range(rays):
        slot = slot_ref[r]
        scene = lax.shift_right_logical(slot, 1)
        turn = jnp.bitwise_and(group_ref[0] - lax.shift_right_logical(scene, 5), 3)
        row = turn * 16 + jnp.bitwise_and(lax.shift_right_logical(scene, 1), 15)
        first = 8 * jnp.bitwise_and(scene, 1) + 3 * jnp.bitwise_and(slot, 1)
        kept = jnp.logical_and(lane >= first, lane < first + 3)
        rows_ref[r : r + 1, :] = jnp.where(kept, tint_ref[row], 0.0)
    turned = rows_ref[...].T
    color_ref[...] = (turned[0:3, :] + turned[3:6, :]) + (turned[8:11, :] + turned[11:14, :])


def finish(group, slot, planes):
    vmem = pl.BlockSpec(memory_space=pltpu.VMEM)
    smem = pl.BlockSpec(memory_space=pltpu.SMEM)
    rays = slot.shape[0]
    return pl.pallas_call(
        finish_kernel,
        out_shape=(
            jax.ShapeDtypeStruct((3, rays), f32),
            jax.ShapeDtypeStruct((1, 1), f32),
            jax.ShapeDtypeStruct((32, 1024), f32),
            jax.ShapeDtypeStruct((8, 128), f32),
        ),
        in_specs=[smem, smem] + [vmem] * 4,
        out_specs=(vmem,) * 4,
        scratch_shapes=[pltpu.VMEM((64, 1, 128), f32), pltpu.VMEM((rays, 128), f32)],
        compiler_params=pltpu.CompilerParams(vmem_limit_bytes=4 * 1024 * 1024),
        cost_estimate=pl.CostEstimate(flops=300_000, bytes_accessed=500_000, transcendentals=0),
        name="finish",
    )(group, slot, *planes)


def body(
    latents,
    head_weight,
    norm_gain,
    color_head,
    sample_points,
    sample_spacing,
    ray_targets,
    ray_scene,
):
    slots = lax.axis_size(both)
    shards = lax.axis_size("shard")
    groups = lax.axis_size("grp")
    core = jnp.bitwise_and(lax.axis_index("shard"), 1).reshape(1).astype(jnp.int32)
    group = lax.axis_index("grp").reshape(1).astype(jnp.int32)
    gain_line = norm_gain[None, :]
    same_core = [[i for i in range(shards) if i % 2 == c] for c in range(2)]
    across = [(i, i ^ 1) for i in range(shards)]

    def among_same_core(x):
        return lax.all_to_all(x, "shard", split_axis=0, concat_axis=0, tiled=True, axis_index_groups=same_core)

    place = jnp.concatenate([group, core])
    *parts, slot = pack(place, ray_scene, sample_points, sample_spacing, ray_targets, slots)
    own_rows = among_same_core(copies(head_weight, shards // 2))
    own_rows = own_rows.reshape(512, 1024)
    for n in range(1, 8):
        moves = [
            (z * shards + i, (z + n // 2) % groups * shards + (i ^ (n % 2))) for z in range(groups) for i in range(shards)
        ]
        parts[n] = lax.ppermute(parts[n], both, moves)
    sent, own_rows = lax.optimization_barrier((stack(place, parts), own_rows))
    other_rows = lax.ppermute(own_rows, "shard", across)
    recv = among_same_core(sent).reshape(slots, 640)
    weight, w0t, w1, w1t, keep, send = make_field(core, latents, own_rows, other_rows, gain_line)
    x_other = lax.ppermute(send, "shard", across)
    colors, d_field = render(recv, w0t, w1, w1t, color_head)
    d_other = lax.ppermute(d_field, "shard", across)
    latent_grad, note = latent_gradient(latents, weight, gain_line, d_field, colors)
    note_other = lax.ppermute(note, "shard", across)
    paired = pair_terms(core, keep, x_other, d_field, d_other, note, note_other)
    planes = plane_sum(group, among_same_core(paired))
    planes = [planes[0]] + [
        lax.ppermute(planes[k], "grp", [(i, (i + k) % groups) for i in range(groups)]) for k in range(1, groups)
    ]
    rendered, loss, head_grad, gain_grad = finish(group, slot, planes)
    return (rendered, loss.reshape(()), head_grad, gain_grad.reshape(-1), latent_grad)


def solution(mesh):
    placed = (
        P(both, None),
        P("shard", None),
        P(),
        P(),
        P(both, None),
        P(both, None),
        P(None, both),
        P(both),
    )
    return jax.shard_map(
        body,
        mesh=mesh,
        in_specs=placed,
        out_specs=(
            P(None, both),
            P(),
            P("shard", None),
            P(),
            P(both, None),
        ),
        check_vma=False,
    )
```

```python
import jax
import jax.numpy as jnp
from jax import lax
from jax.experimental import pallas as pl
from jax.experimental.pallas import tpu as pltpu
from jax.sharding import PartitionSpec as P

norm_eps = 1e-06
f32, bf16 = jnp.float32, jnp.bfloat16
both = ("grp", "shard")

sin_coef = (3.141590256747904, -5.167405766362, 2.544000216186916, -0.5594350008327638)
cos_coef = (0.999999953027512, -4.934792802489427, 4.058410790762133, -1.3318729727851486, 0.21968242357146)

step_block = 8
features = 48


def fold_matrix():
    m = lax.broadcasted_iota(jnp.int32, (features, 256), 0).astype(f32)
    i = lax.broadcasted_iota(jnp.int32, (features, 256), 1).astype(f32)
    q = jnp.floor(i * (1 / 64) + 1 / 128)
    j = 4.0 * (i - 64.0 * q) + q
    jm = j - features * jnp.floor((j + 0.5) * (1 / features))
    coordinate = jnp.floor((m + 0.5) * (1 / 16))
    phase = jnp.floor((m - 16.0 * coordinate + 0.5) * (1 / 8))
    octave = m - 16.0 * coordinate - 8.0 * phase
    return (jm == coordinate + 3.0 * phase + 6.0 * octave).astype(f32)


def dot(a, b, dims=(((1,), (0,)), ((), ())), precision=None):
    return lax.dot_general(a, b, dims, preferred_element_type=f32, precision=precision)


def pack_kernel(place_ref, scene_ref, points_ref, spacing_ref, target_ref, *rest):
    outs, (slot_ref, count_ref, row_ref, pay_ref, tint_ref) = rest[:8], rest[8:]
    rays = points_ref.shape[0]
    group, core = place_ref[0], place_ref[1]
    for d in range(count_ref.shape[0]):
        count_ref[d] = 0
    row_ref[...] = jnp.zeros_like(row_ref)
    pay_ref[:, 0:192] = points_ref[...]
    pay_ref[:, 192:256] = spacing_ref[...]
    target = jnp.concatenate([target_ref[...], jnp.zeros((5, rays), f32)], axis=0).T
    lane = lax.broadcasted_iota(jnp.int32, (rays, 128), 1)
    for k in range(2):
        placed = jnp.zeros((rays, 128), f32)
        for c in range(3):
            placed = jnp.where(lane == 3 * k + c, target[:, c : c + 1], placed)
        tint_ref[k] = placed

    for r in range(rays):
        scene = scene_ref[r]
        rank = count_ref[scene]
        count_ref[scene] = rank + 1
        slot_ref[r] = scene * 2 + rank
        turn = jnp.bitwise_and(lax.shift_right_logical(scene, 5) - group, 3)
        side = jnp.bitwise_and(scene + core, 1)
        row = (turn * 2 + side) * 16 + jnp.bitwise_and(lax.shift_right_logical(scene, 1), 15)
        row_ref[row, :, pl.ds(pl.multiple_of(rank * 256, 256), 256)] = pay_ref[r : r + 1, :]
        row_ref[row, :, 512:640] += tint_ref[rank, r : r + 1, :]
    for n, out in enumerate(outs):
        out[...] = row_ref[n * 16 : (n + 1) * 16]


def pack(place, ray_scene, points, spacing, targets, slots):
    rays = points.shape[0]
    smem = pl.BlockSpec(memory_space=pltpu.SMEM)
    vmem = pl.BlockSpec(memory_space=pltpu.VMEM)
    return pl.pallas_call(
        pack_kernel,
        out_shape=(
            *(jax.ShapeDtypeStruct((slots // 8, 1, 640), f32),) * 8,
            jax.ShapeDtypeStruct((rays,), jnp.int32),
        ),
        in_specs=[smem, smem] + [vmem] * 3,
        out_specs=(*(vmem,) * 8, smem),
        scratch_shapes=[
            pltpu.SMEM((slots,), jnp.int32),
            pltpu.VMEM((slots, 1, 640), f32),
            pltpu.VMEM((rays, 256), f32),
            pltpu.VMEM((2, rays, 128), f32),
        ],
        compiler_params=pltpu.CompilerParams(vmem_limit_bytes=4 * 1024 * 1024),
        cost_estimate=pl.CostEstimate(flops=200000, bytes_accessed=1000000, transcendentals=0),
        name="pack",
    )(place, ray_scene, points, spacing, targets)


def stack_kernel(place_ref, *rest):
    parts, out_ref = rest[:8], rest[8]
    group, core = place_ref[0], place_ref[1]
    for n, part in enumerate(parts):
        source = jnp.bitwise_and(group - n // 2, 3) * 2 + jnp.bitwise_and(core + n, 1)
        for i in range(16):
            out_ref[i, source] = part[i]


def stack(place, parts):
    vmem = pl.BlockSpec(memory_space=pltpu.VMEM)
    return pl.pallas_call(
        stack_kernel,
        out_shape=jax.ShapeDtypeStruct((16, 8, 1, 640), f32),
        in_specs=[pl.BlockSpec(memory_space=pltpu.SMEM)] + [vmem] * 8,
        out_specs=vmem,
        compiler_params=pltpu.CompilerParams(vmem_limit_bytes=4 * 1024 * 1024),
        cost_estimate=pl.CostEstimate(flops=100_000, bytes_accessed=800_000, transcendentals=0),
        name="stack",
    )(place, *parts)


def copies_kernel(rows_ref, out_ref):
    rows = rows_ref[...]
    for i in range(out_ref.shape[0]):
        out_ref[i] = rows


def copies(rows, count):
    vmem = pl.BlockSpec(memory_space=pltpu.VMEM)
    return pl.pallas_call(
        copies_kernel,
        out_shape=jax.ShapeDtypeStruct((count, *rows.shape), rows.dtype),
        in_specs=[vmem],
        out_specs=vmem,
        compiler_params=pltpu.CompilerParams(vmem_limit_bytes=4 * 1024 * 1024),
        cost_estimate=pl.CostEstimate(flops=0, bytes_accessed=1_000_000, transcendentals=0),
        name="copies",
    )(rows)


def field_kernel(
    core_ref,
    latent_ref,
    own_ref,
    other_ref,
    gain_ref,
    weight_ref,
    w0t_ref,
    w1_ref,
    w1t_ref,
    keep_ref,
    send_ref,
    hat_ref,
    inv_ref,
    rows_ref,
    turned_ref,
):
    scale = 1.0 / 16.0
    own = core_ref[0]
    for i in range(16):
        for part, ref in ((own, own_ref), (1 - own, other_ref)):
            weight_ref[pl.ds(pl.multiple_of(i * 64 + part * 32, 32), 32), :] = ref[i * 32 : (i + 1) * 32, :]
    latent = latent_ref[...].astype(f32)
    inv_rms = lax.rsqrt(jnp.mean(latent * latent, axis=1, keepdims=True) + norm_eps)
    hat_ref[...] = latent * inv_rms
    inv_ref[...] = jnp.broadcast_to(inv_rms, inv_ref.shape)
    normed = latent * inv_rms * gain_ref[...]
    field = dot(normed.astype(bf16), weight_ref[...]).astype(bf16)
    stacked = jnp.concatenate([field[0:64, q * 256 : (q + 1) * 256] for q in range(4)], axis=0)
    folded = dot(fold_matrix().astype(bf16), stacked) * scale
    high = folded.astype(bf16).astype(f32)
    split = jnp.concatenate([high, folded - high, jnp.zeros((32, 256), f32)], axis=0)
    w0t_ref[...] = split.T.astype(bf16)
    field1 = field[64:128, :].astype(f32) * scale
    for q in range(4):
        for n in range(2):
            rows_ref[n, pl.ds(q, 64, stride=4), :] = field1[:, q * 256 + n * 128 : q * 256 + (n + 1) * 128]
    w1f = jnp.concatenate([rows_ref[0], rows_ref[1]], axis=1)
    w1_ref[...] = w1f.astype(bf16)
    w1t_ref[...] = w1f.T.astype(bf16)
    turned_ref[...] = normed.T.astype(bf16)
    for out, part in ((keep_ref, own), (send_ref, 1 - own)):
        for i in range(16):
            out[i * 32 : (i + 1) * 32, :] = turned_ref[pl.ds(pl.multiple_of(i * 64 + part * 32, 32), 32), :]


def make_field(core, latents, own_rows, other_rows, gain):
    vmem = pl.BlockSpec(memory_space=pltpu.VMEM)
    shapes = ((1024, 1024), (256, 128), (256, 256), (256, 256), (512, 128), (512, 128))
    return pl.pallas_call(
        field_kernel,
        out_shape=(
            *(jax.ShapeDtypeStruct(shape, bf16) for shape in shapes),
            jax.ShapeDtypeStruct((128, 1024), f32),
            jax.ShapeDtypeStruct((128, 128), f32),
        ),
        in_specs=[pl.BlockSpec(memory_space=pltpu.SMEM)] + [vmem] * 4,
        out_specs=(vmem,) * 8,
        scratch_shapes=[pltpu.VMEM((2, 256, 128), f32), pltpu.VMEM((1024, 128), bf16)],
        compiler_params=pltpu.CompilerParams(vmem_limit_bytes=24 * 1024 * 1024),
        cost_estimate=pl.CostEstimate(flops=400_000_000, bytes_accessed=5_000_000, transcendentals=0),
        name="field",
    )(core, latents, own_rows, other_rows, gain)


def horner(u, coef):
    value = coef[-1] * u + coef[-2]
    for c in coef[-3::-1]:
        value = value * u + c
    return value


def render_kernel(
    recv_ref,
    w0t_ref,
    w1_ref,
    w1t_ref,
    head_ref,
    color_ref,
    dfield_ref,
    rays_ref,
    h0_ref,
    h1_ref,
    h2_ref,
    raw_ref,
    draw_ref,
    g0_ref,
    g1_ref,
    rows_ref,
):
    scale = 1.0 / 16.0
    slots = recv_ref.shape[0]
    rays = 2 * slots
    blocks = 64 // step_block

    for k in range(2):
        rays_ref[0:256, k * slots : (k + 1) * slots] = recv_ref[:, k * 256 : (k + 1) * 256].T
    tint = recv_ref[:, 512:640].T
    w0t = w0t_ref[:, 0:96]
    w1 = w1_ref[...]
    w1t = w1t_ref[...]
    head_f = jnp.concatenate([head_ref[...].astype(f32), jnp.zeros((4, 256), f32)], axis=0)
    head = head_f.astype(bf16)
    head_t = (head_f * scale).T.astype(bf16)

    octave = jnp.left_shift(1, lax.broadcasted_iota(jnp.int32, (8, rays), 0)).astype(f32)

    def forward(b, carry):
        parts = [[] for _ in range(6)]
        for c in range(3):
            group = rays_ref[pl.ds(pl.multiple_of(c * 64 + b * step_block, 8), step_block), :]
            for s in range(step_block):
                y = group[s : s + 1, :] * octave
                whole = jnp.floor(y + 0.5)
                r = y - whole
                half = whole * 0.5
                sign = 1.0 - 4.0 * (half - jnp.floor(half))
                u = r * r
                parts[2 * c].append(r * sign * horner(u, sin_coef))
                parts[2 * c + 1].append(sign * horner(u, cos_coef))
        h0 = jnp.concatenate([jnp.concatenate(p, axis=1) for p in parts], axis=0).astype(bf16)
        h0_ref[b] = h0
        h1 = jnp.maximum(dot(w0t, jnp.concatenate([h0, h0], axis=0)), 0.0).astype(bf16)
        h1_ref[b] = h1
        h2 = jnp.maximum(dot(w1t, h1), 0.0).astype(bf16)
        h2_ref[b] = h2
        raw = dot(head, h2)
        for s in range(step_block):
            at = pl.ds(pl.multiple_of((b * step_block + s) * 8, 8), 8)
            for k in range(2):
                raw_ref[k, at, :] = raw[:, (2 * s + k) * slots : (2 * s + k + 1) * slots]
        return carry

    lax.fori_loop(0, blocks, forward, 0, unroll=True)

    def spread(c):
        return jnp.concatenate([raw_ref[k, pl.ds(c, 64, stride=8), :] for k in range(2)], axis=1)

    def store_gradient(c, value):
        for k in range(2):
            draw_ref[k, pl.ds(c, 64, stride=8), :] = value[:, k * slots : (k + 1) * slots]

    spacing = rays_ref[192:256, :]
    row = lax.broadcasted_iota(jnp.int32, (64, 64), 0)
    column = lax.broadcasted_iota(jnp.int32, (64, 64), 1)
    raw0 = spread(0)
    density = jnp.maximum(raw0, 0.0) + jnp.log1p(jnp.exp(-jnp.abs(raw0)))
    optical = density * spacing
    before = dot((column < row).astype(f32), optical, precision=lax.Precision.HIGHEST)
    transmit = jnp.exp(-before)
    survive = jnp.exp(-optical)
    blend = transmit * (1.0 - survive)
    live = (spacing[0:1, :] > 0.0).astype(f32)
    factor = 1.0 / (float(slots) * jnp.sum(live, axis=1, keepdims=True))
    albedo = [jax.nn.sigmoid(spread(1 + c)) for c in range(3)]
    d_blend = jnp.zeros_like(blend)
    square = jnp.zeros_like(live)
    colors, grads = [], []
    for c in range(3):
        color = jnp.sum(blend * (albedo[c] - 1.0), axis=0, keepdims=True) + 1.0
        target = jnp.concatenate([tint[c : c + 1, :], tint[3 + c : 4 + c, :]], axis=1)
        residual = (color - target) * live
        square = square + residual * residual
        grad = 2.0 * residual * factor
        d_blend = d_blend + grad * (albedo[c] - 1.0)
        colors.append(color)
        grads.append(grad)
    loss = jnp.sum(square, axis=1, keepdims=True) * factor
    rows = [colors[c][:, k * slots : (k + 1) * slots] for k in range(2) for c in range(3)]
    color_ref[...] = jnp.concatenate([*rows, jnp.broadcast_to(loss, (2, slots))], axis=0)
    weighted = d_blend * blend
    behind = dot((column > row).astype(f32), weighted, precision=lax.Precision.HIGHEST)
    d_optical = d_blend * transmit * survive - behind
    draw_ref[...] = jnp.zeros_like(draw_ref)
    store_gradient(0, d_optical * spacing * jax.nn.sigmoid(raw0))
    for c in range(3):
        store_gradient(1 + c, grads[c] * blend * albedo[c] * (1.0 - albedo[c]))

    g0_ref[...] = jnp.zeros_like(g0_ref)
    g1_ref[...] = jnp.zeros_like(g1_ref)
    on_lanes = (((1,), (1,)), ((), ()))

    def backward(b, carry):
        d_raw = jnp.concatenate(
            [
                draw_ref[k, pl.ds(pl.multiple_of((b * step_block + s) * 8, 8), 8), :]
                for s in range(step_block)
                for k in range(2)
            ],
            axis=1,
        ).astype(bf16)
        h1 = h1_ref[b]
        d_a2 = jnp.where(h2_ref[b] > 0, dot(head_t, d_raw).astype(bf16), jnp.zeros((), bf16))
        d_a1 = jnp.where(h1 > 0, dot(w1, d_a2).astype(bf16), jnp.zeros((), bf16))
        g1_ref[...] += dot(h1, d_a2, on_lanes)
        g0_ref[...] += dot(h0_ref[b], d_a1, on_lanes)
        return carry

    lax.fori_loop(0, blocks, backward, 0, unroll=True)

    unfold = jnp.concatenate([fold_matrix(), jnp.zeros((80, 256), f32)], axis=0).T[:, 0:features].astype(bf16)
    g0 = dot(unfold, g0_ref[...].astype(bf16)).astype(bf16)
    for n in range(2):
        rows_ref[n] = g1_ref[:, n * 128 : (n + 1) * 128]
    for q in range(4):
        dfield_ref[0:64, q * 256 : (q + 1) * 256] = g0[q * 64 : (q + 1) * 64, :]
        for n in range(2):
            at = slice(q * 256 + n * 128, q * 256 + (n + 1) * 128)
            dfield_ref[64:128, at] = rows_ref[n, pl.ds(q, 64, stride=4), :].astype(bf16)


def render(recv, w0t, w1, w1t, head):
    slots = recv.shape[0]
    rays = 2 * slots
    blocks, wide = 64 // step_block, step_block * rays
    vmem = pl.BlockSpec(memory_space=pltpu.VMEM)
    return pl.pallas_call(
        render_kernel,
        out_shape=(
            jax.ShapeDtypeStruct((8, slots), f32),
            jax.ShapeDtypeStruct((128, 1024), bf16),
        ),
        in_specs=[vmem] * 5,
        out_specs=(vmem,) * 2,
        scratch_shapes=[
            pltpu.VMEM((256, rays), f32),
            pltpu.VMEM((blocks, features, wide), bf16),
            pltpu.VMEM((blocks, 256, wide), bf16),
            pltpu.VMEM((blocks, 256, wide), bf16),
            pltpu.VMEM((2, 512, slots), f32),
            pltpu.VMEM((2, 512, slots), f32),
            pltpu.VMEM((features, 256), f32),
            pltpu.VMEM((256, 256), f32),
            pltpu.VMEM((2, 256, 128), f32),
        ],
        compiler_params=pltpu.CompilerParams(vmem_limit_bytes=44 * 1024 * 1024),
        cost_estimate=pl.CostEstimate(flops=12_000_000_000, bytes_accessed=2_000_000, transcendentals=1_000_000),
        name="render",
    )(recv, w0t, w1, w1t, head)


def latent_kernel(hat_ref, inv_ref, weight_ref, gain_ref, dfield_ref, color_ref, out_ref, note_ref):
    x_hat = hat_ref[...]
    inv_rms = inv_ref[:, 0:1]
    d_norm = dot(dfield_ref[...], weight_ref[...], (((1,), (1,)), ((), ())))
    term = d_norm * x_hat
    gain = jnp.sum(term, axis=0, keepdims=True)
    mean = jnp.mean(term * gain_ref[...], axis=1, keepdims=True)
    out_ref[...] = (inv_rms * (d_norm * gain_ref[...] - x_hat * mean)).astype(bf16)
    note_ref[0:8, :] = color_ref[...]
    for i in range(8):
        note_ref[8 + i : 9 + i, :] = gain[:, i * 128 : (i + 1) * 128]


def latent_gradient(x_hat, inv_rms, weight, gain, d_field, colors):
    vmem = pl.BlockSpec(memory_space=pltpu.VMEM)
    return pl.pallas_call(
        latent_kernel,
        out_shape=(
            jax.ShapeDtypeStruct(x_hat.shape, bf16),
            jax.ShapeDtypeStruct((16, 128), f32),
        ),
        in_specs=[vmem] * 6,
        out_specs=(vmem,) * 2,
        compiler_params=pltpu.CompilerParams(vmem_limit_bytes=24 * 1024 * 1024),
        cost_estimate=pl.CostEstimate(flops=300_000_000, bytes_accessed=3_000_000, transcendentals=0),
        name="latent_gradient",
    )(x_hat, inv_rms, weight, gain, d_field, colors)


def two_terms(value):
    high = value.astype(bf16).astype(f32)
    return high, value - high


def pair_kernel(
    core_ref, keep_ref, other_ref, dfield_ref, dother_ref, note_ref, nother_ref, out_ref, turned_ref
):
    first = core_ref[0] == 0
    mine, mate = note_ref[...], nother_ref[...]
    colors = jnp.concatenate(
        [jnp.where(first, mine, mate)[0:8, :], jnp.where(first, mate, mine)[0:8, :], jnp.zeros((112, 128), f32)],
        axis=0,
    )
    turned_ref[...] = colors.T
    gain = two_terms(mine[8:16, :] + mate[8:16, :])
    x_both = jnp.concatenate([keep_ref[...], other_ref[...]], axis=1)
    d_both = jnp.concatenate([dfield_ref[...], dother_ref[...]], axis=0)
    terms = dot(x_both, d_both).astype(bf16)
    for i in range(16):
        out_ref[i, :, 0:1024] = terms[i * 32 : (i + 1) * 32, :]
        rows = [turned_ref[pl.ds(8 * i + c, 4, stride=2), :] for c in range(2)]
        tint = two_terms(jnp.where(first, *rows))
        out_ref[i, :, 1024:1152] = jnp.concatenate(
            [*tint, *gain, jnp.zeros((8, 128), f32)], axis=0
        ).astype(bf16)


def pair_terms(core, keep, other, d_field, d_other, note, note_other):
    vmem = pl.BlockSpec(memory_space=pltpu.VMEM)
    return pl.pallas_call(
        pair_kernel,
        out_shape=jax.ShapeDtypeStruct((16, 32, 1152), bf16),
        in_specs=[pl.BlockSpec(memory_space=pltpu.SMEM)] + [vmem] * 6,
        out_specs=vmem,
        scratch_shapes=[pltpu.VMEM((128, 128), f32)],
        compiler_params=pltpu.CompilerParams(vmem_limit_bytes=16 * 1024 * 1024),
        cost_estimate=pl.CostEstimate(flops=270_000_000, bytes_accessed=2_000_000, transcendentals=0),
        name="pair_terms",
    )(core, keep, other, d_field, d_other, note, note_other)


def plane_kernel(group_ref, terms_ref, *rest):
    outs, tint_ref = rest[:4], rest[4]
    total = terms_ref[0, :, 0:1024].astype(f32)
    gain = jnp.zeros((8, 128), f32)
    for i in range(terms_ref.shape[0]):
        if i:
            total = total + terms_ref[i, :, 0:1024].astype(f32)
        extra = terms_ref[i, :, 1024:1152].astype(f32)
        gain = gain + (extra[8:16, :] + extra[16:24, :])
        tint = extra[0:4, :] + extra[4:8, :]
        for z in range(4):
            tint_ref[z, i : i + 1, :] = tint[z : z + 1, :]
    total = total.astype(bf16)
    gain_rows = jnp.concatenate([*two_terms(gain), jnp.zeros((16, 128), f32)], axis=0).astype(bf16)
    for k, out in enumerate(outs):
        out[:, 0:1024] = total
        tint = tint_ref[jnp.bitwise_and(group_ref[0] + k, 3)]
        out[:, 1024:1152] = jnp.concatenate(two_terms(tint), axis=0).astype(bf16)
        out[:, 1152:1280] = gain_rows


def plane_sum(group, terms):
    vmem = pl.BlockSpec(memory_space=pltpu.VMEM)
    return pl.pallas_call(
        plane_kernel,
        out_shape=(jax.ShapeDtypeStruct((32, 1280), bf16),) * 4,
        in_specs=[pl.BlockSpec(memory_space=pltpu.SMEM), vmem],
        out_specs=(vmem,) * 4,
        scratch_shapes=[pltpu.VMEM((4, 16, 128), f32)],
        compiler_params=pltpu.CompilerParams(vmem_limit_bytes=8 * 1024 * 1024),
        cost_estimate=pl.CostEstimate(flops=1_000_000, bytes_accessed=1_500_000, transcendentals=0),
        name="plane_sum",
    )(group, terms)


def finish_kernel(group_ref, slot_ref, m0, m1, m2, m3, color_ref, loss_ref, head_ref, gain_out_ref, tint_ref, rows_ref):
    rays = color_ref.shape[1]
    planes = (m0, m1, m2, m3)

    def summed(parts):
        return (parts[0] + parts[2]) + (parts[1] + parts[3])

    head_ref[...] = summed([m[:, 0:1024].astype(f32) for m in planes])
    gains = [m[:, 1152:1280].astype(f32) for m in planes]
    gain_out_ref[...] = summed([g[0:8, :] + g[8:16, :] for g in gains])
    losses = []
    for k, m in enumerate(planes):
        tint = m[:, 1024:1152].astype(f32)
        tint = tint[0:16, :] + tint[16:32, :]
        losses.append(jnp.sum(tint, axis=0, keepdims=True))
        for i in range(16):
            tint_ref[k * 16 + i] = tint[i : i + 1, :]
    lane = lax.broadcasted_iota(jnp.int32, (1, 128), 1)
    loss = jnp.where(jnp.logical_or(lane == 6, lane == 14), summed(losses), 0.0)
    loss_ref[...] = jnp.sum(loss, axis=1, keepdims=True)
    for r in range(rays):
        slot = slot_ref[r]
        scene = lax.shift_right_logical(slot, 1)
        turn = jnp.bitwise_and(group_ref[0] - lax.shift_right_logical(scene, 5), 3)
        row = turn * 16 + jnp.bitwise_and(lax.shift_right_logical(scene, 1), 15)
        first = 8 * jnp.bitwise_and(scene, 1) + 3 * jnp.bitwise_and(slot, 1)
        kept = jnp.logical_and(lane >= first, lane < first + 3)
        rows_ref[r : r + 1, :] = jnp.where(kept, tint_ref[row], 0.0)
    turned = rows_ref[...].T
    color_ref[...] = (turned[0:3, :] + turned[3:6, :]) + (turned[8:11, :] + turned[11:14, :])


def finish(group, slot, planes):
    vmem = pl.BlockSpec(memory_space=pltpu.VMEM)
    smem = pl.BlockSpec(memory_space=pltpu.SMEM)
    rays = slot.shape[0]
    return pl.pallas_call(
        finish_kernel,
        out_shape=(
            jax.ShapeDtypeStruct((3, rays), f32),
            jax.ShapeDtypeStruct((1, 1), f32),
            jax.ShapeDtypeStruct((32, 1024), f32),
            jax.ShapeDtypeStruct((8, 128), f32),
        ),
        in_specs=[smem, smem] + [vmem] * 4,
        out_specs=(vmem,) * 4,
        scratch_shapes=[pltpu.VMEM((64, 1, 128), f32), pltpu.VMEM((rays, 128), f32)],
        compiler_params=pltpu.CompilerParams(vmem_limit_bytes=4 * 1024 * 1024),
        cost_estimate=pl.CostEstimate(flops=300_000, bytes_accessed=500_000, transcendentals=0),
        name="finish",
    )(group, slot, *planes)


def body(
    latents,
    head_weight,
    norm_gain,
    color_head,
    sample_points,
    sample_spacing,
    ray_targets,
    ray_scene,
):
    slots = lax.axis_size(both)
    shards = lax.axis_size("shard")
    groups = lax.axis_size("grp")
    core = jnp.bitwise_and(lax.axis_index("shard"), 1).reshape(1).astype(jnp.int32)
    group = lax.axis_index("grp").reshape(1).astype(jnp.int32)
    gain_line = norm_gain[None, :]
    same_core = [[i for i in range(shards) if i % 2 == c] for c in range(2)]
    across = [(i, i ^ 1) for i in range(shards)]

    def among_same_core(x):
        return lax.all_to_all(x, "shard", split_axis=0, concat_axis=0, tiled=True, axis_index_groups=same_core)

    place = jnp.concatenate([group, core])
    *parts, slot = pack(place, ray_scene, sample_points, sample_spacing, ray_targets, slots)
    own_rows = among_same_core(copies(head_weight, shards // 2))
    own_rows = own_rows.reshape(512, 1024)
    for n in range(1, 8):
        moves = [
            (z * shards + i, (z + n // 2) % groups * shards + (i ^ (n % 2))) for z in range(groups) for i in range(shards)
        ]
        parts[n] = lax.ppermute(parts[n], both, moves)
    sent, own_rows = lax.optimization_barrier((stack(place, parts), own_rows))
    other_rows = lax.ppermute(own_rows, "shard", across)
    recv = among_same_core(sent).reshape(slots, 640)
    weight, w0t, w1, w1t, keep, send, x_hat, inv_rms = make_field(core, latents, own_rows, other_rows, gain_line)
    x_other = lax.ppermute(send, "shard", across)
    colors, d_field = render(recv, w0t, w1, w1t, color_head)
    d_other = lax.ppermute(d_field, "shard", across)
    latent_grad, note = latent_gradient(x_hat, inv_rms, weight, gain_line, d_field, colors)
    note_other = lax.ppermute(note, "shard", across)
    paired = pair_terms(core, keep, x_other, d_field, d_other, note, note_other)
    planes = plane_sum(group, among_same_core(paired))
    planes = [planes[0]] + [
        lax.ppermute(planes[k], "grp", [(i, (i + k) % groups) for i in range(groups)]) for k in range(1, groups)
    ]
    rendered, loss, head_grad, gain_grad = finish(group, slot, planes)
    return (rendered, loss.reshape(()), head_grad, gain_grad.reshape(-1), latent_grad)


def solution(mesh):
    placed = (
        P(both, None),
        P("shard", None),
        P(),
        P(),
        P(both, None),
        P(both, None),
        P(None, both),
        P(both),
    )
    return jax.shard_map(
        body,
        mesh=mesh,
        in_specs=placed,
        out_specs=(
            P(None, both),
            P(),
            P("shard", None),
            P(),
            P(both, None),
        ),
        check_vma=False,
    )
```
